128 devices in a mesh: val: 4 (over z_lo, core), cond: 32 (over y, x, z_hi).
Axes of the slice: x: 4, y: 4, z: 4 (z_hi: 2, z_lo: 2; z = z_hi * 2 + z_lo), core: 2. Of those that a mesh axis runs over, the one named last changes fastest.
Arguments:
- valence_orbitals: bfloat16 [8, 96, 9216], P('val', 'cond'), may hold values from -6 to 6
- conduction_orbitals: bfloat16 [256, 96, 9216], P('cond'), may hold values from -6 to 6
- valence_energy: float32 [8], P('val'), may hold values from -14 to -5
- conduction_energy: float32 [256], P('cond'), may hold values from 0.5 to 40
- sphere_index: int32 [4096], replicated, may hold values from 0 to 884735, as said below
Outputs:
- polar_real: float32 [4096, 4096], P('cond', 'val')
- polar_imag: float32 [4096, 4096], P('cond', 'val')
The draws below stay inside these ranges and needn't reach their ends.
Inputs may be any that keep to these rules, and one draw needn't show every extreme that they name: `sphere_index`: distinct flat indices (a * 96 + b) * 96 + e of the grid: the 4096 frequency vectors nearest the anchor, ties in length broken at random, listed in random order. Each component a, b, e, read as a frequency in -48 to 47, lies within -10 to 10.
All inputs are finite; a program needn't handle non-finite values.
Results may differ from the reference program's by a relative error of at most 0.0003.
Values may be sent and summed in bfloat16 or wider, within the bound.
No kernel may reach another device: no remote copies, remote signals or barrier semaphores. Data moves between devices by JAX's collectives and lax.ppermute only.
A program may use at most 320 MiB of HBM per device.

```python
import math
import jax
import jax.numpy as jnp
from jax import lax

NGRID = 96
KCUT = 10
NG = 4096
NVAL = 8
NCOND = 256


def draw_sphere_index(key, part):
    key = jax.random.fold_in(key, 11)
    tie_key = jax.random.fold_in(key, 1)
    order_key = jax.random.fold_in(key, 2)
    side = 2 * KCUT + 1
    total = side * side * side
    cells = jnp.arange(total, dtype=jnp.int32)
    first = cells // (side * side) - KCUT
    second = cells // side % side - KCUT
    third = cells % side - KCUT
    radius = first * first + second * second + third * third
    breaker = jax.random.permutation(tie_key, total).astype(jnp.int32)
    scores = radius * total + breaker
    chosen = jnp.argsort(scores, stable=True)[:NG]
    chosen = chosen[jax.random.permutation(order_key, NG)]
    flat = (first[chosen] % NGRID * NGRID + second[chosen] % NGRID) * NGRID + third[chosen] % NGRID
    return flat.astype(jnp.int32)


def level_of(rng, shape, split, low, largest):
    gain = 1.0
    for axis_at, blocks in split:
        heights = jax.random.uniform(jax.random.fold_in(jax.random.fold_in(rng, 6), axis_at), (blocks,), jnp.float32, low / len(split), largest / len(split))
        gain = gain * jnp.repeat(jnp.exp(heights), shape[axis_at] // blocks).reshape((-1,) + (1,) * (len(shape) - 1 - axis_at))
    return gain


def centred(key, dims, scale, reach, pieces=(), kind=jnp.bfloat16):
    values = jax.random.normal(key, dims, jnp.float32) * scale
    if len(pieces) > 0:
        values = level_of(key, dims, pieces, -0.22, 0.18) * values
    return jnp.clip(values, min=-reach, max=reach).astype(kind)


def setup_inputs(seed: int = 0) -> dict:
    key_of = jax.random.split(jax.random.key(seed), 6)
    valence_orbitals = centred(key_of[0], (NVAL, NGRID, NGRID * NGRID), 1.0, 6.0, ((0, 4), (1, 32)))
    conduction_orbitals = centred(key_of[1], (NCOND, NGRID, NGRID * NGRID), 1.0, 6.0, ((0, 32),))
    valence_energy = jnp.clip(-14.0 + 9.0 * jax.random.uniform(key_of[2], (NVAL,), jnp.float32) ** level_of(key_of[2], (NVAL,), ((0, 4),), -0.2, 0.2), -14.0, -5.0)
    conduction_energy = jnp.clip(jnp.exp(math.log(40.0) - 4.3820266 * jax.random.uniform(key_of[3], (NCOND,), jnp.float32) ** level_of(key_of[3], (NCOND,), ((0, 32),), -0.2, 0.2)), 0.5, 40.0)
    sphere_index = draw_sphere_index(jax.random.fold_in(key_of[5], 71), 0)
    return {"valence_orbitals": valence_orbitals, "conduction_orbitals": conduction_orbitals, "valence_energy": valence_energy, "conduction_energy": conduction_energy, "sphere_index": sphere_index}


def twiddles(extent, cutoff):
    frequency = jnp.arange(2 * cutoff + 1, dtype=jnp.int32) - cutoff
    positions = jnp.arange(extent, dtype=jnp.int32)
    phases = (positions[:, None] * (frequency[None, :] % extent)) % extent
    angles = phases.astype(jnp.float32) * (2.0 * math.pi / extent)
    return jnp.cos(angles), jnp.sin(angles)


def transform_yz(density, extent, cutoff):
    cosines, sine_part = twiddles(extent, cutoff)
    width = cosines.shape[1]
    table_zed = jnp.concatenate([cosines, -sine_part], axis=1)
    along_z = jnp.einsum("bxyz,zl->bxyl", density, table_zed, precision=lax.Precision.HIGHEST)
    table_yed = jnp.concatenate([cosines, sine_part], axis=1)
    products = jnp.einsum("bxyj,yl->bxlj", along_z, table_yed, precision=lax.Precision.HIGHEST)
    real_part = products[:, :, :width, :width] + products[:, :, width:, width:]
    imag_part = products[:, :, :width, width:] - products[:, :, width:, :width]
    return jnp.stack([real_part, imag_part], axis=1)


def finish_x(partial_value, extent, cutoff):
    cosines, sine_part = twiddles(extent, cutoff)
    width = cosines.shape[1]
    table_xed = jnp.concatenate([cosines, sine_part], axis=1)
    products = jnp.einsum("bsxac,xl->bslac", partial_value, table_xed, precision=lax.Precision.HIGHEST)
    real_part = products[:, 0, :width] + products[:, 1, width:]
    imag_part = products[:, 1, :width] - products[:, 0, width:]
    factor = float(extent) ** -1.5
    count = partial_value.shape[0]
    return real_part.reshape(count, -1) * factor, imag_part.reshape(count, -1) * factor


def sphere_cells(sphere_index, extent, cutoff):
    side = 2 * cutoff + 1
    first = sphere_index // (extent * extent)
    second = (sphere_index // extent) % extent
    third = sphere_index % extent

    def folded(values):
        return jnp.where(values >= extent // 2, values - extent, values) + cutoff

    return ((folded(first) * side + folded(second)) * side + folded(third)).astype(jnp.int32)


def reference(valence_orbitals, conduction_orbitals, valence_energy, conduction_energy, sphere_index):
    cells = sphere_cells(sphere_index, NGRID, KCUT)
    blocks = conduction_orbitals.reshape(NCOND // 8, 8, NGRID, NGRID * NGRID)

    def one_valence(orbital):
        def one_block(group):
            density = orbital.astype(jnp.float32)[None] * group.astype(jnp.float32)
            density = density.reshape(8, NGRID, NGRID, NGRID)
            real_part, imag_part = finish_x(transform_yz(density, NGRID, KCUT), NGRID, KCUT)
            return jnp.concatenate([jnp.take(real_part, cells, axis=1), jnp.take(imag_part, cells, axis=1)], axis=1)

        return lax.map(one_block, blocks)

    coefs = lax.map(one_valence, valence_orbitals).reshape(NVAL * NCOND, 2 * NG)
    weights = (2.0 / (valence_energy[:, None] - conduction_energy[None, :])).reshape(-1)
    row_side = coefs * weights[:, None]
    products = lax.dot_general(row_side, coefs, (((0,), (0,)), ((), ())), precision=lax.Precision.HIGHEST)
    factor = float(NVAL * NCOND) ** -0.5
    polar_real = (products[:NG, :NG] + products[NG:, NG:]) * factor
    polar_imag = (products[NG:, :NG] - products[:NG, NG:]) * factor
    return polar_real, polar_imag
```

```python
import math

import jax
import jax.numpy as jnp
import numpy as np
from jax import lax
from jax.experimental import pallas as pl
from jax.experimental.pallas import tpu as pltpu
from jax.sharding import Mesh, PartitionSpec as P

NGRID = 96
KCUT = 10
NG = 4096
SIDE = 2 * KCUT + 1
HALF = NGRID // 2
PLANE = NGRID * NGRID
FOLD = PLANE // 2
ELEN = KCUT + 1
CHUNK = 512
PAIRS = 16
CODES = 32767.0
LOG2 = math.log(2.0)
VAL = ("zl", "core")
COND = ("y", "x", "zh")


def split_np(table):
    high = table.astype(jnp.bfloat16)
    low = (table - high.astype(np.float64)).astype(jnp.bfloat16)
    return high, low


def plane_tables():
    phase_y = np.arange(HALF)[:, None, None, None]
    phase_z = np.arange(NGRID)[None, :, None, None]
    zed = np.arange(ELEN)[None, None, None, :]
    blocks = []
    for first in (-KCUT, -KCUT + 1):
        yed = np.arange(first, KCUT + 1, 2)[None, None, :, None]
        angle = (yed * phase_y + zed * phase_z) % NGRID * (2.0 * math.pi / NGRID)
        angle = angle.reshape(FOLD, -1)
        table = np.zeros((FOLD, 256))
        table[:, : angle.shape[1]] = np.cos(angle)
        table[:, 128 : 128 + angle.shape[1]] = -np.sin(angle)
        blocks.append(table)
    even_high, even_low = split_np(blocks[0])
    odd_high, odd_low = split_np(blocks[1])
    return even_high, even_low, odd_high, odd_low


def line_tables():
    freq = np.arange(-KCUT, KCUT + 1)[:, None]
    angle = freq * np.arange(NGRID)[None, :] % NGRID * (2.0 * math.pi / NGRID)
    parts = np.stack([np.cos(angle), np.sin(angle)])
    eye = np.eye(PAIRS)
    table = np.einsum("sax,pq->sapqx", parts, eye)
    return split_np(table.reshape(2 * SIDE * PAIRS, PAIRS * NGRID))


def dot32(left, right):
    return lax.dot_general(
        left, right, (((1,), (0,)), ((), ())), preferred_element_type=jnp.float32
    )


def split(value):
    high = value.astype(jnp.bfloat16)
    low = (value - high.astype(jnp.float32)).astype(jnp.bfloat16)
    return high, low


def plane_kernel(v0_ref, v1_ref, c0_ref, c1_ref, eh_ref, el_ref, oh_ref, ol_ref, out_ref):
    first = pl.program_id(0) == 0

    @pl.when(first)
    def _():
        out_ref[...] = jnp.zeros_like(out_ref)

    vcount = v0_ref.shape[0]
    ccount = c0_ref.shape[0]
    group = 4
    for v in range(vcount):
        v0 = v0_ref[v].astype(jnp.float32)[None]
        v1 = v1_ref[v].astype(jnp.float32)[None]
        for c in range(0, ccount, group):
            d0 = v0 * c0_ref[c : c + group].astype(jnp.float32)
            d1 = v1 * c1_ref[c : c + group].astype(jnp.float32)
            rows = group * d0.shape[1]
            at = (v * ccount + c) * d0.shape[1]
            for which, value in enumerate((d0 + d1, d0 - d1)):
                high, low = split(value.reshape(rows, CHUNK))
                th = (eh_ref, oh_ref)[which][...]
                tl = (el_ref, ol_ref)[which][...]
                part = dot32(high, th) + dot32(low, th) + dot32(high, tl)
                out_ref[at : at + rows, which * 256 : which * 256 + 256] += part


def plane_transform(valence, conduction, tables):
    vcount, planes, _ = valence.shape
    ccount = conduction.shape[0]
    steps = FOLD // CHUNK
    rows = vcount * ccount * planes
    vspec = lambda off: pl.BlockSpec((vcount, planes, CHUNK), lambda k: (0, 0, k + off))
    cspec = lambda off: pl.BlockSpec((ccount, planes, CHUNK), lambda k: (0, 0, k + off))
    tspec = pl.BlockSpec((CHUNK, 256), lambda k: (k, 0))
    return pl.pallas_call(
        plane_kernel,
        grid=(steps,),
        in_specs=[vspec(0), vspec(steps), cspec(0), cspec(steps)] + [tspec] * 4,
        out_specs=pl.BlockSpec((rows, 512), lambda k: (0, 0)),
        out_shape=jax.ShapeDtypeStruct((rows, 512), jnp.float32),
        compiler_params=pltpu.CompilerParams(vmem_limit_bytes=56 * 2**20),
        cost_estimate=pl.CostEstimate(
            flops=rows * FOLD * 512 * 6, bytes_accessed=40 * 2**20, transcendentals=0
        ),
        name="plane_transform",
    )(valence, valence, conduction, conduction, *tables)


def line_kernel(
    y_ref, th_ref, tl_ref, lane_ref, freq_ref, sign_ref, gain_ref, cols_ref, rows_ref, step_ref,
    fh_ref, fl_ref, coef_ref,
):
    high, low = split(y_ref[...])
    th = th_ref[...]
    both = dot32(th, high) + dot32(th, low) + dot32(tl_ref[...], high)
    rows = SIDE * PAIRS
    cosine, sine = both[:rows], both[rows:]
    for par in range(2):
        at = par * 256
        real = cosine[:, at : at + 128] + sine[:, at + 128 : at + 256]
        imag = cosine[:, at + 128 : at + 256] - sine[:, at : at + 128]
        lanes = slice(par * 128, par * 128 + 128)
        fh_ref[:rows, lanes], fl_ref[:rows, lanes] = split(real)
        fh_ref[rows:, lanes], fl_ref[rows:, lanes] = split(imag)
    width = 512
    gain = gain_ref[...]

    def pick(tile, largest):
        cols = pl.ds(pl.multiple_of(tile * width, width), width)
        lane = lane_ref[:, cols]
        onehot = lax.broadcasted_iota(jnp.int32, (256, width), 0) == lane
        onehot = onehot.astype(jnp.float32).astype(jnp.bfloat16)
        freq = freq_ref[:, cols]
        picked = dot32(fh_ref[...], onehot) + dot32(fl_ref[...], onehot)
        for part in range(2):
            total = jnp.zeros((PAIRS, width), jnp.float32)
            for a in range(SIDE):
                at = part * rows + a * PAIRS
                total = jnp.where(freq == a, picked[at : at + PAIRS], total)
            total = total * gain
            if part == 1:
                total = total * sign_ref[:, cols]
            coef_ref[part * PAIRS : (part + 1) * PAIRS, cols] = total
            largest = jnp.maximum(largest, jnp.max(jnp.abs(total), axis=1, keepdims=True))
        return largest

    largest = lax.fori_loop(0, NG // width, pick, jnp.zeros((PAIRS, 1), jnp.float32))
    usable = largest > 1e-30
    step = jnp.ceil(jnp.log(jnp.where(usable, largest, 1.0) * (1.0 / CODES)) * (1.0 / LOG2))
    step_ref[...] = jnp.broadcast_to(step, step_ref.shape)
    inverse = jnp.where(usable, jnp.exp(step * -LOG2), 0.0)
    inverse = jnp.concatenate([inverse, inverse])
    for block in range(32):
        codes = jnp.round(coef_ref[:, block * 128 : (block + 1) * 128] * inverse)
        codes = jnp.clip(codes, -CODES, CODES).astype(jnp.int32).astype(jnp.int16)
        rows_ref[block] = codes
        cols_ref[block // 8, :, block % 8 * 128 : block % 8 * 128 + 128] = codes


def line_transform(planes, tables, slots, gain):
    rows = 2 * SIDE * PAIRS
    return pl.pallas_call(
        line_kernel,
        out_shape=(
            jax.ShapeDtypeStruct((4, 2 * PAIRS, NG // 4), jnp.int16),
            jax.ShapeDtypeStruct((32, 2 * PAIRS, NG // 32), jnp.int16),
            jax.ShapeDtypeStruct((PAIRS, 128), jnp.float32),
        ),
        scratch_shapes=[pltpu.VMEM((rows, 256), jnp.bfloat16)] * 2
        + [pltpu.VMEM((2 * PAIRS, NG), jnp.float32)],
        compiler_params=pltpu.CompilerParams(vmem_limit_bytes=48 * 2**20),
        cost_estimate=pl.CostEstimate(
            flops=rows * (PAIRS * NGRID * 512 * 6 + 256 * NG * 4),
            bytes_accessed=8 * 2**20,
            transcendentals=0,
        ),
        name="line_transform",
    )(planes, *tables, *slots, gain)


def pair_kernel(cols_ref, rows_ref, scale_ref, real_ref, imag_ref, total_ref):
    step = pl.program_id(0)
    depth = cols_ref.shape[0]
    rows = rows_ref.shape[1]
    row = rows_ref[...].astype(jnp.float32) * scale_ref[...]
    block = row.reshape(depth // (2 * PAIRS), 2, PAIRS, rows)
    turned = jnp.concatenate([block[:, 1:], -block[:, :1]], axis=1).reshape(depth, rows)
    rh, rl = split(jnp.concatenate([row, turned], axis=1))
    code = cols_ref[...].astype(jnp.int32)
    top = jnp.right_shift(code + 128, 8) * 256
    high = top.astype(jnp.float32).astype(jnp.bfloat16)
    low = (code - top).astype(jnp.float32).astype(jnp.bfloat16)

    def contract(left, right):
        return lax.dot_general(
            left, right, (((0,), (0,)), ((), ())), preferred_element_type=jnp.float32
        )

    part = contract(rh, high) + contract(rl, high) + contract(rh, low)

    @pl.when(step == 0)
    def _():
        total_ref[...] = part

    @pl.when(step > 0)
    def _():
        total_ref[...] += part

    @pl.when(step == pl.num_programs(0) - 1)
    def _():
        real_ref[...] = total_ref[:rows]
        imag_ref[...] = total_ref[rows:]


def pair_product(cols, rows, scale):
    depth = 512
    count, width = cols.shape
    height = rows.shape[1]
    shape = jax.ShapeDtypeStruct((height, width), jnp.float32)
    spec = lambda size: pl.BlockSpec((depth, size), lambda k: (k, 0))
    out = pl.BlockSpec((height, width), lambda k: (0, 0))
    return pl.pallas_call(
        pair_kernel,
        grid=(count // depth,),
        in_specs=[spec(width), spec(height), spec(1)],
        out_specs=(out, out),
        out_shape=(shape, shape),
        scratch_shapes=[pltpu.VMEM((2 * height, width), jnp.float32)],
        compiler_params=pltpu.CompilerParams(vmem_limit_bytes=48 * 2**20),
        cost_estimate=pl.CostEstimate(
            flops=6 * 2 * height * width * count, bytes_accessed=12 * 2**20, transcendentals=0
        ),
        name="pair_product",
    )(cols, rows, scale)


def sphere_slots(sphere_index):
    def folded(values):
        return jnp.where(values >= HALF, values - NGRID, values)

    first = folded(sphere_index // PLANE)
    second = folded(sphere_index // NGRID % NGRID)
    third = folded(sphere_index % NGRID)
    flip = third < 0
    sign = jnp.where(flip, -1, 1)
    first, second, third = first * sign, second * sign, third * sign
    even = second % 2 == 0
    lane = jnp.where(
        even, (second + KCUT) // 2 * ELEN + third, 128 + (second + KCUT - 1) // 2 * ELEN + third
    )
    row = lambda value: value.reshape(1, NG)
    return row(lane), row(first + KCUT), row(sign.astype(jnp.float32))


def gather_planes(orbitals):
    count = orbitals.shape[0]
    mine = orbitals.reshape(-1, 128).astype(jnp.float32)
    rows = mine.shape[0]
    largest = jnp.max(jnp.abs(mine))
    power = jnp.where(largest > 0.0, jnp.ceil(jnp.log2(jnp.where(largest > 0.0, largest, 1.0))), 0.0)
    power = jnp.maximum(power, -100.0)
    packed = jnp.concatenate(
        [mine * jnp.exp2(-power), jnp.broadcast_to(power, (8, 128))]
    ).astype(jnp.float16)
    packed = lax.all_gather(packed, "zh", axis=0)
    packed = lax.all_gather(packed, ("y", "x"), axis=0)
    values = packed[:, :, :rows].astype(jnp.float32)
    values = values * jnp.exp2(packed[:, :, rows:rows + 1, :1].astype(jnp.float32))
    values = values.astype(jnp.bfloat16).reshape(32, count, -1, 72, 128)
    return jnp.swapaxes(values, 0, 1).reshape(count, NGRID, PLANE)


def columns_of_all(coded):
    twice = jnp.broadcast_to(coded, (2,) + coded.shape).reshape((8,) + coded.shape[1:])
    line = lax.all_to_all(twice, ("zh",) + VAL, 0, 0, tiled=True)
    return lax.all_gather(line, ("y", "x"), axis=0).reshape(-1, coded.shape[-1])


def rows_of_all(coded, steps):
    height, rows = coded.shape[1:]
    steps = jnp.pad(steps[:, 0].astype(jnp.int16)[None], ((0, 7), (0, rows - PAIRS)))
    sent = jnp.concatenate([coded, jnp.broadcast_to(steps, (32, 8, rows))], axis=1)
    sent = jnp.broadcast_to(sent, (4,) + sent.shape).reshape((128,) + sent.shape[1:])
    got = lax.all_to_all(sent, VAL + COND, 0, 0, tiled=True)
    got = got.reshape(4, 16, 2, height + 8, rows).transpose(1, 2, 0, 3, 4)
    scale = jnp.exp2(2.0 * got[..., height, :PAIRS].astype(jnp.float32))
    scale = jnp.concatenate([scale, scale], axis=-1).reshape(-1, 1)
    return got[..., :height, :].reshape(-1, rows), -scale


def per_device(
    valence_orbitals, conduction_orbitals, valence_energy, conduction_energy, sphere_index
):
    slots = sphere_slots(sphere_index)
    weights = 2.0 / (conduction_energy[None, :] - valence_energy[:, None])
    gain = jnp.sqrt(weights * 2048.0**-0.5) * float(NGRID) ** -1.5
    valence = gather_planes(valence_orbitals)
    planes = plane_transform(valence, conduction_orbitals, plane_tables())
    cols, rows, steps = line_transform(planes, line_tables(), slots, gain.reshape(-1, 1))
    rows, scale = rows_of_all(rows, steps)
    return pair_product(columns_of_all(cols), rows, scale)


def solution(mesh):
    names = ("zl", "core", "y", "x", "zh")
    fine = Mesh(mesh.devices.reshape(2, 2, 4, 4, 2), names)
    placed = (P(VAL, COND, None), P(COND, None, None), P(VAL), P(COND), P())
    return jax.shard_map(
        per_device,
        mesh=fine,
        in_specs=placed,
        out_specs=(P(COND, VAL), P(COND, VAL)),
        check_vma=False,
    )
```

```python
import math

import jax
import jax.numpy as jnp
import numpy as np
from jax import lax
from jax.experimental import pallas as pl
from jax.experimental.pallas import tpu as pltpu
from jax.sharding import Mesh, PartitionSpec as P

NGRID = 96
KCUT = 10
NG = 4096
SIDE = 2 * KCUT + 1
HALF = NGRID // 2
PLANE = NGRID * NGRID
FOLD = PLANE // 2
ELEN = KCUT + 1
CHUNK = 512
PAIRS = 16
GROUP = 8
ROWS = 176
CODES = 32767.0
LOG2 = math.log(2.0)
VAL = ("zl", "core")
COND = ("y", "x", "zh")


def split_np(table):
    high = table.astype(jnp.bfloat16)
    low = (table - high.astype(np.float64)).astype(jnp.bfloat16)
    return high, low


def plane_tables():
    phase_y = np.arange(HALF)[:, None, None, None]
    phase_z = np.arange(NGRID)[None, :, None, None]
    zed = np.arange(ELEN)[None, None, None, :]
    blocks = []
    for first in (-KCUT, -KCUT + 1):
        yed = np.arange(first, KCUT + 1, 2)[None, None, :, None]
        angle = (yed * phase_y + zed * phase_z) % NGRID * (2.0 * math.pi / NGRID)
        angle = angle.reshape(FOLD, -1)
        table = np.zeros((FOLD, 256))
        table[:, : angle.shape[1]] = np.cos(angle)
        table[:, 128 : 128 + angle.shape[1]] = -np.sin(angle)
        blocks.append(table)
    even_high, even_low = split_np(blocks[0])
    odd_high, odd_low = split_np(blocks[1])
    return even_high, even_low, odd_high, odd_low


def line_tables():
    freq = np.arange(-KCUT, KCUT + 1)[:, None]
    angle = freq * np.arange(NGRID)[None, :] % NGRID * (2.0 * math.pi / NGRID)
    parts = np.stack([np.cos(angle), np.sin(angle)])
    eye = np.eye(GROUP)
    table = np.einsum("sax,pq->sapqx", parts, eye)
    return split_np(table.reshape(2 * SIDE * GROUP, GROUP * NGRID))


def dot32(left, right):
    return lax.dot_general(
        left, right, (((1,), (0,)), ((), ())), preferred_element_type=jnp.float32
    )


def split(value):
    high = value.astype(jnp.bfloat16)
    low = (value - high.astype(jnp.float32)).astype(jnp.bfloat16)
    return high, low


def decode(code):
    code = code.astype(jnp.int32)
    size = jnp.abs(code) - 1
    scale = jnp.exp2((jnp.right_shift(size, 7) - 133).astype(jnp.float32))
    value = (jnp.bitwise_and(size, 127) + 128).astype(jnp.float32) * scale
    return jnp.where(code == 0, 0.0, jnp.where(code < 0, -value, value))


def add_planes(v_ref, c0_ref, c1_ref, eh_ref, el_ref, oh_ref, ol_ref, value_ref, plane_ref):
    planes = value_ref.shape[0]
    value_ref[...] = decode(v_ref[...]).reshape(value_ref.shape)
    ccount = c0_ref.shape[0]
    vcount = PAIRS // ccount
    group = 4
    lines = CHUNK // 128
    rows = group * planes
    halves = [
        [
            jnp.concatenate(
                [value_ref[:, (2 * v + half) * lines + r, :] for r in range(lines)], axis=1
            )[None]
            for half in range(2)
        ]
        for v in range(vcount)
    ]
    for c in range(0, ccount, group):
        c0 = c0_ref[c : c + group].astype(jnp.float32)
        c1 = c1_ref[c : c + group].astype(jnp.float32)
        for v in range(vcount):
            d0, d1 = halves[v][0] * c0, halves[v][1] * c1
            at = (v * ccount + c) * planes
            for which, value in enumerate((d0 + d1, d0 - d1)):
                high, low = split(value.reshape(rows, CHUNK))
                th = (eh_ref, oh_ref)[which][...]
                tl = (el_ref, ol_ref)[which][...]
                both = dot32(jnp.concatenate([high, low]), th)
                part = both[:rows] + both[rows:] + dot32(high, tl)
                plane_ref[at : at + rows, which * 256 : which * 256 + 256] += part


def finish_pairs(
    plane_ref, th_ref, tl_ref, index_ref, valence_ref, conduction_ref,
    cols_ref, rows_ref, step_ref, fold_ref, coef_ref,
):
    th, tl = th_ref[...], tl_ref[...]
    used = SIDE * GROUP
    groups = PAIRS // GROUP
    for group in range(groups):
        depth = GROUP * NGRID
        high, low = split(plane_ref[group * depth : (group + 1) * depth])
        both = dot32(th, high) + dot32(th, low) + dot32(tl, high)
        cosine, sine = both[:used], both[used:]
        for par in range(2):
            at = par * 256
            real = cosine[:, at : at + 128] + sine[:, at + 128 : at + 256]
            imag = cosine[:, at + 128 : at + 256] - sine[:, at : at + 128]
            for part, value in enumerate((real, imag)):
                first = (part * groups + group) * ROWS
                value = jnp.concatenate([value, jnp.zeros((ROWS - used, 128), jnp.float32)])
                high_part, low_part = split(value)
                fold_ref[first : first + ROWS, par * 128 : par * 128 + 128] = high_part
                fold_ref[first : first + ROWS, 256 + par * 128 : 384 + par * 128] = low_part
    width = 512
    gain = pair_gain(valence_ref, conduction_ref, conduction_ref.shape[0])

    def pick(tile, largest):
        cols = pl.ds(pl.multiple_of(tile * width, width), width)
        lane, freq, sign = sphere_slots(index_ref[:, cols])
        onehot = lax.broadcasted_iota(jnp.int32, (256, width), 0) == lane
        onehot = onehot.astype(jnp.float32).astype(jnp.bfloat16)
        picked = dot32(fold_ref[...], jnp.concatenate([onehot, onehot]))
        totals = [jnp.zeros((GROUP, width), jnp.float32)] * (2 * groups)
        for a in range(SIDE):
            here = freq == a
            for at in range(2 * groups):
                first = at * ROWS + a * GROUP
                totals[at] = jnp.where(here, picked[first : first + GROUP], totals[at])
        for part in range(2):
            total = jnp.concatenate(totals[part * groups : (part + 1) * groups]) * gain
            if part == 1:
                total = total * sign
            coef_ref[part * PAIRS : (part + 1) * PAIRS, cols] = total
            largest = jnp.maximum(largest, jnp.max(jnp.abs(total), axis=1, keepdims=True))
        return largest

    largest = lax.fori_loop(0, NG // width, pick, jnp.zeros((PAIRS, 1), jnp.float32))
    usable = largest > 1e-30
    step = jnp.ceil(jnp.log(jnp.where(usable, largest, 1.0) * (1.0 / CODES)) * (1.0 / LOG2))
    lane = lax.broadcasted_iota(jnp.int32, step_ref.shape, 1)
    powers = jnp.where(lane % 2 == 0, step, jnp.concatenate([step[8:], step[:8]]))
    step_ref[...] = powers.astype(jnp.int32).astype(jnp.int16)
    inverse = jnp.where(usable, jnp.exp2(-step), 0.0)
    inverse = jnp.concatenate([inverse, inverse])
    for block in range(32):
        codes = jnp.round(coef_ref[:, block * 128 : (block + 1) * 128] * inverse)
        codes = jnp.clip(codes, -CODES, CODES).astype(jnp.int32).astype(jnp.int16)
        rows_ref[block] = codes
        for half in range(2):
            at = half * 4 + block // 8
            cols_ref[at, :, block % 8 * 128 : block % 8 * 128 + 128] = codes


def coefficient_kernel(*refs):
    streamed, constant = refs[:7], refs[7:12]
    outputs = refs[12:15]
    value_ref, plane_ref, fold_ref, coef_ref = refs[15:]

    @pl.when(pl.program_id(0) == 0)
    def _():
        plane_ref[...] = jnp.zeros_like(plane_ref)

    add_planes(*streamed, value_ref, plane_ref)

    @pl.when(pl.program_id(0) == pl.num_programs(0) - 1)
    def _():
        finish_pairs(plane_ref, *constant, *outputs, fold_ref, coef_ref)


def pair_coefficients(valence, conduction, plane_part, line_part, index, energies):
    owners, steps, mine, lines, _ = valence.shape
    planes = owners * mine
    ccount = conduction.shape[0]
    rows = PAIRS * planes
    vspec = pl.BlockSpec((owners, 1, mine, lines, 128), lambda k: (0, k, 0, 0, 0))
    cspec = lambda off: pl.BlockSpec((ccount, planes, CHUNK), lambda k: (0, 0, k + off))
    tspec = pl.BlockSpec((CHUNK, 256), lambda k: (k, 0))
    whole = lambda shape: pl.BlockSpec(shape, lambda k: (0,) * len(shape))
    constant = [*line_part, index.reshape(1, -1)]
    scalar = pl.BlockSpec(memory_space=pltpu.SMEM)
    shapes = ((8, 2 * PAIRS, NG // 4), (32, 2 * PAIRS, NG // 32), (PAIRS, 128))
    kinds = (jnp.int16, jnp.int16, jnp.int16)
    return pl.pallas_call(
        coefficient_kernel,
        grid=(steps,),
        in_specs=[vspec, cspec(0), cspec(steps)]
        + [tspec] * 4
        + [whole(value.shape) for value in constant]
        + [scalar, scalar],
        out_specs=tuple(whole(shape) for shape in shapes),
        out_shape=tuple(jax.ShapeDtypeStruct(*both) for both in zip(shapes, kinds)),
        scratch_shapes=[
            pltpu.VMEM((planes, lines, 128), jnp.float32),
            pltpu.VMEM((rows, 512), jnp.float32),
            pltpu.VMEM((2 * (PAIRS // GROUP) * ROWS, 512), jnp.bfloat16),
            pltpu.VMEM((2 * PAIRS, NG), jnp.float32),
        ],
        compiler_params=pltpu.CompilerParams(vmem_limit_bytes=56 * 2**20),
        cost_estimate=pl.CostEstimate(
            flops=rows * FOLD * 512 * 6, bytes_accessed=40 * 2**20, transcendentals=0
        ),
        name="pair_coefficients",
    )(valence, conduction, conduction, *plane_part, *constant, *energies)


def pair_kernel(cols_ref, rows_ref, real_ref, imag_ref, total_ref):
    step = pl.program_id(0)
    values, lines, heights, height, rows = rows_ref.shape
    pieces = []
    for y in range(lines):
        for h in range(heights):
            for v in range(values):
                block = rows_ref[v, y, h].astype(jnp.float32)
                scale = -jnp.exp2(2.0 * block[2 * PAIRS :])
                block = jnp.concatenate(
                    [block[at * 8 : at * 8 + 8] * scale[:, at : at + 1] for at in range(4)]
                )
                turned = jnp.concatenate([block[PAIRS:], -block[:PAIRS]])
                pieces.append(jnp.concatenate([block, turned], axis=1))
    high, low = split(jnp.concatenate(pieces).T)
    both = jnp.concatenate([high, low])
    ch, cl = split(cols_ref[...].astype(jnp.float32))
    part = dot32(both, ch)
    part = part[: 2 * rows] + part[2 * rows :] + dot32(high, cl)

    @pl.when(step == 0)
    def _():
        total_ref[...] = part

    @pl.when(step > 0)
    def _():
        total_ref[...] += part

    @pl.when(step == pl.num_programs(0) - 1)
    def _():
        real_ref[...] = total_ref[:rows]
        imag_ref[...] = total_ref[rows:]


def pair_product(cols, rows):
    count, width = cols.shape
    values, lines, heights, height, short = rows.shape
    each = 4
    depth = count // lines * each
    shape = jax.ShapeDtypeStruct((short, width), jnp.float32)
    out = pl.BlockSpec((short, width), lambda k: (0, 0))
    return pl.pallas_call(
        pair_kernel,
        grid=(lines // each,),
        in_specs=[
            pl.BlockSpec((depth, width), lambda k: (k, 0)),
            pl.BlockSpec((values, each, heights, height, short), lambda k: (0, k, 0, 0, 0)),
        ],
        out_specs=(out, out),
        out_shape=(shape, shape),
        scratch_shapes=[pltpu.VMEM((2 * short, width), jnp.float32)],
        compiler_params=pltpu.CompilerParams(vmem_limit_bytes=48 * 2**20),
        cost_estimate=pl.CostEstimate(
            flops=6 * 2 * short * width * count, bytes_accessed=12 * 2**20, transcendentals=0
        ),
        name="pair_product",
    )(cols, rows)


def sphere_slots(index):
    def quotient(value, divisor):
        exact = (value.astype(jnp.float32) + 0.5) * (1.0 / divisor)
        return jnp.floor(exact).astype(jnp.int32)

    def folded(value):
        return jnp.where(value >= HALF, value - NGRID, value)

    first = quotient(index, PLANE)
    rest = index - first * PLANE
    second = quotient(rest, NGRID)
    third = folded(rest - second * NGRID)
    first, second = folded(first), folded(second)
    sign = jnp.where(third < 0, -1, 1)
    first, second, third = first * sign, second * sign, third * sign
    turn = second + KCUT
    lane = jnp.right_shift(turn, 1) * ELEN + third + jnp.bitwise_and(turn, 1) * 128
    return lane, first + KCUT, sign.astype(jnp.float32)


def pair_gain(valence_ref, conduction_ref, ccount):
    at = lax.broadcasted_iota(jnp.int32, (PAIRS, 1), 0)
    gap = jnp.zeros((PAIRS, 1), jnp.float32)
    for pair in range(PAIRS):
        this = conduction_ref[pair % ccount] - valence_ref[pair // ccount]
        gap = jnp.where(at == pair, this, gap)
    return jnp.sqrt(2.0 / gap * 2048.0**-0.5) * float(NGRID) ** -1.5


def encode(values):
    size = jnp.abs(values.astype(jnp.float32))
    tiny = size < 2.0**-126
    size = jnp.where(tiny, 1.0, size)
    power = jnp.floor(jnp.log2(size))
    code = (power + 126.0) * 128.0 + jnp.round((size * jnp.exp2(-power) - 1.0) * 128.0) + 1.0
    return jnp.where(tiny, 0.0, jnp.where(values < 0, -code, code)).astype(jnp.int16)


def gather_planes(orbitals):
    count, mine = orbitals.shape[:2]
    lines = CHUNK // 128
    steps = FOLD // CHUNK
    codes = encode(orbitals).reshape(count, mine, 2, steps, lines, 128)
    codes = jnp.transpose(codes, (3, 1, 0, 2, 4, 5)).reshape(-1, 128)
    codes = lax.all_gather(codes, "zh", axis=0)
    codes = lax.all_gather(codes, ("y", "x"), axis=0)
    return codes.reshape(32, steps, mine, 2 * count * lines, 128)


def columns_and_rows(cols, rows, steps):
    height, short = rows.shape[1:]
    sent = jnp.concatenate(
        [
            jnp.broadcast_to(rows, (4,) + rows.shape),
            jnp.broadcast_to(steps[:8], (4, 32, 8, short)),
        ],
        axis=2,
    ).reshape(128, height + 8, short)
    sent = lax.all_to_all(sent, VAL + COND, 0, 0, tiled=True)
    line = lax.all_to_all(cols, ("zh",) + VAL, 0, 0, tiled=True)
    cols = lax.all_gather(line, ("y", "x"), axis=0).reshape(-1, cols.shape[-1])
    return cols, sent.reshape(4, 16, 2, height + 8, short)


def per_device(
    valence_orbitals, conduction_orbitals, valence_energy, conduction_energy, sphere_index
):
    coded = pair_coefficients(
        gather_planes(valence_orbitals),
        conduction_orbitals,
        plane_tables(),
        line_tables(),
        sphere_index,
        (valence_energy, conduction_energy),
    )
    return pair_product(*columns_and_rows(*coded))


def solution(mesh):
    names = ("zl", "core", "y", "x", "zh")
    fine = Mesh(mesh.devices.reshape(2, 2, 4, 4, 2), names)
    placed = (P(VAL, COND, None), P(COND, None, None), P(VAL), P(COND), P())
    return jax.shard_map(
        per_device,
        mesh=fine,
        in_specs=placed,
        out_specs=(P(COND, VAL), P(COND, VAL)),
        check_vma=False,
    )
```

```python
import math

import jax
import jax.numpy as jnp
import numpy as np
from jax import lax
from jax.experimental import pallas as pl
from jax.experimental.pallas import tpu as pltpu
from jax.sharding import Mesh, PartitionSpec as P

NGRID = 96
KCUT = 10
NG = 4096
SIDE = 2 * KCUT + 1
HALF = NGRID // 2
PLANE = NGRID * NGRID
FOLD = PLANE // 2
ELEN = KCUT + 1
CHUNK = 512
PAIRS = 16
GROUP = 8
ROWS = 176
CODES = 32767.0
LOG2 = math.log(2.0)
VAL = ("zl", "core")
COND = ("y", "x", "zh")


def split_np(table):
    high = table.astype(jnp.bfloat16)
    low = (table - high.astype(np.float64)).astype(jnp.bfloat16)
    return high, low


def plane_tables():
    phase_y = np.arange(HALF)[:, None, None, None]
    phase_z = np.arange(NGRID)[None, :, None, None]
    zed = np.arange(ELEN)[None, None, None, :]
    blocks = []
    for first in (-KCUT, -KCUT + 1):
        yed = np.arange(first, KCUT + 1, 2)[None, None, :, None]
        angle = (yed * phase_y + zed * phase_z) % NGRID * (2.0 * math.pi / NGRID)
        angle = angle.reshape(FOLD, -1)
        table = np.zeros((FOLD, 256))
        table[:, : angle.shape[1]] = np.cos(angle)
        table[:, 128 : 128 + angle.shape[1]] = -np.sin(angle)
        blocks.append(table)
    even_high, even_low = split_np(blocks[0])
    odd_high, odd_low = split_np(blocks[1])
    return even_high, even_low, odd_high, odd_low


def line_tables():
    freq = np.arange(-KCUT, KCUT + 1)[:, None]
    angle = freq * np.arange(NGRID)[None, :] % NGRID * (2.0 * math.pi / NGRID)
    parts = np.stack([np.cos(angle), np.sin(angle)])
    eye = np.eye(GROUP)
    table = np.einsum("sax,pq->sapqx", parts, eye)
    return split_np(table.reshape(2 * SIDE * GROUP, GROUP * NGRID))


def dot32(left, right):
    return lax.dot_general(
        left, right, (((1,), (0,)), ((), ())), preferred_element_type=jnp.float32
    )


def split(value):
    high = value.astype(jnp.bfloat16)
    low = (value - high.astype(jnp.float32)).astype(jnp.bfloat16)
    return high, low


def decode(code):
    code = code.astype(jnp.int32)
    scale = jnp.exp2(jnp.right_shift(code, 8).astype(jnp.float32))
    low = jnp.bitwise_and(code, 255).astype(jnp.float32)
    return jnp.where(low < 128.0, low + 128.0, -low) * scale


def add_planes(v_ref, c0_ref, c1_ref, eh_ref, el_ref, oh_ref, ol_ref, value_ref, plane_ref):
    vcount, each, planes = value_ref.shape[:3]
    values = decode(v_ref[...]).reshape(planes, vcount * each, 128)
    for v in range(vcount):
        value_ref[v] = jnp.swapaxes(values[:, v * each : (v + 1) * each], 0, 1)
    ccount = c0_ref.shape[0]
    group, each = 4, 16
    lines = CHUNK // 128
    rows = group * planes
    for c in range(0, ccount, group):
        for v in range(vcount):
            parts = [[], []], [[], []]
            for band in range(c, c + group):
                for first in range(0, planes, each):
                    here = slice(first, first + each)
                    d0, d1 = (
                        jnp.concatenate(
                            [value_ref[v, half * lines + r, here] for r in range(lines)], axis=1
                        )
                        * c_ref[band, here].astype(jnp.float32)
                        for half, c_ref in enumerate((c0_ref, c1_ref))
                    )
                    for which, value in enumerate((d0 + d1, d0 - d1)):
                        for part, value in zip(parts[which], split(value)):
                            part.append(value)
            at = (v * ccount + c) * planes
            for which, (highs, lows) in enumerate(parts):
                th = (eh_ref, oh_ref)[which][...]
                tl = (el_ref, ol_ref)[which][...]
                both = dot32(jnp.concatenate(highs + lows), th)
                part = both[:rows] + both[rows:] + dot32(jnp.concatenate(highs), tl)
                plane_ref[at : at + rows, which * 256 : which * 256 + 256] += part


def finish_pairs(
    plane_ref, th_ref, tl_ref, index_ref, valence_ref, conduction_ref,
    cols_ref, rows_ref, step_ref, fold_ref, coef_ref,
):
    th, tl = th_ref[...], tl_ref[...]
    used = SIDE * GROUP
    groups = PAIRS // GROUP
    for group in range(groups):
        depth = GROUP * NGRID
        high, low = split(plane_ref[group * depth : (group + 1) * depth])
        both = dot32(th, high) + dot32(th, low) + dot32(tl, high)
        cosine, sine = both[:used], both[used:]
        for par in range(2):
            at = par * 256
            real = cosine[:, at : at + 128] + sine[:, at + 128 : at + 256]
            imag = cosine[:, at + 128 : at + 256] - sine[:, at : at + 128]
            for part, value in enumerate((real, imag)):
                first = (part * groups + group) * ROWS
                value = jnp.concatenate([value, jnp.zeros((ROWS - used, 128), jnp.float32)])
                high_part, low_part = split(value)
                fold_ref[first : first + ROWS, par * 128 : par * 128 + 128] = high_part
                fold_ref[first : first + ROWS, 256 + par * 128 : 384 + par * 128] = low_part
    width = 512
    gain = pair_gain(valence_ref, conduction_ref, conduction_ref.shape[0])

    def pick(tile, largest):
        cols = slice(tile * width, (tile + 1) * width)
        lane, freq, sign = sphere_slots(index_ref[:, cols])
        onehot = lax.broadcasted_iota(jnp.int32, (256, width), 0) == lane
        onehot = onehot.astype(jnp.float32).astype(jnp.bfloat16)
        picked = dot32(fold_ref[...], jnp.concatenate([onehot, onehot]))
        totals = [jnp.zeros((GROUP, width), jnp.float32)] * (2 * groups)
        for a in range(SIDE):
            here = freq == a
            for at in range(2 * groups):
                first = at * ROWS + a * GROUP
                totals[at] = jnp.where(here, picked[first : first + GROUP], totals[at])
        for part in range(2):
            total = jnp.concatenate(totals[part * groups : (part + 1) * groups]) * gain
            if part == 1:
                total = total * sign
            coef_ref[part * PAIRS : (part + 1) * PAIRS, cols] = total
            largest = jnp.maximum(largest, jnp.max(jnp.abs(total), axis=1, keepdims=True))
        return largest

    largest = jnp.zeros((PAIRS, 1), jnp.float32)
    for tile in range(NG // width):
        largest = pick(tile, largest)
    usable = largest > 1e-30
    step = jnp.ceil(jnp.log(jnp.where(usable, largest, 1.0) * (1.0 / CODES)) * (1.0 / LOG2))
    lane = lax.broadcasted_iota(jnp.int32, step_ref.shape, 1)
    powers = jnp.where(lane % 2 == 0, step, jnp.concatenate([step[8:], step[:8]]))
    step_ref[...] = powers.astype(jnp.int32).astype(jnp.int16)
    inverse = jnp.where(usable, jnp.exp2(-step), 0.0)
    inverse = jnp.concatenate([inverse, inverse])
    for block in range(32):
        codes = jnp.round(coef_ref[:, block * 128 : (block + 1) * 128] * inverse)
        codes = jnp.clip(codes, -CODES, CODES).astype(jnp.int32).astype(jnp.int16)
        rows_ref[block] = codes
        for half in range(2):
            at = half * 4 + block // 8
            cols_ref[at, :, block % 8 * 128 : block % 8 * 128 + 128] = codes


def coefficient_kernel(*refs):
    streamed, constant = refs[:7], refs[7:12]
    outputs = refs[12:15]
    value_ref, plane_ref, fold_ref, coef_ref = refs[15:]

    @pl.when(pl.program_id(0) == 0)
    def _():
        plane_ref[...] = jnp.zeros_like(plane_ref)

    add_planes(*streamed, value_ref, plane_ref)

    @pl.when(pl.program_id(0) == pl.num_programs(0) - 1)
    def _():
        finish_pairs(plane_ref, *constant, *outputs, fold_ref, coef_ref)


def pair_coefficients(valence, conduction, plane_part, line_part, index, energies):
    owners, steps, mine, lines, _ = valence.shape
    planes = owners * mine
    ccount = conduction.shape[0]
    rows = PAIRS * planes
    vspec = pl.BlockSpec((owners, 1, mine, lines, 128), lambda k: (0, k, 0, 0, 0))
    cspec = lambda off: pl.BlockSpec((ccount, planes, CHUNK), lambda k: (0, 0, k + off))
    tspec = pl.BlockSpec((CHUNK, 256), lambda k: (k, 0))
    whole = lambda shape: pl.BlockSpec(shape, lambda k: (0,) * len(shape))
    constant = [*line_part, index.reshape(1, -1)]
    scalar = pl.BlockSpec(memory_space=pltpu.SMEM)
    shapes = ((8, 2 * PAIRS, NG // 4), (32, 2 * PAIRS, NG // 32), (PAIRS, 128))
    kinds = (jnp.int16, jnp.int16, jnp.int16)
    return pl.pallas_call(
        coefficient_kernel,
        grid=(steps,),
        in_specs=[vspec, cspec(0), cspec(steps)]
        + [tspec] * 4
        + [whole(value.shape) for value in constant]
        + [scalar, scalar],
        out_specs=tuple(whole(shape) for shape in shapes),
        out_shape=tuple(jax.ShapeDtypeStruct(*both) for both in zip(shapes, kinds)),
        scratch_shapes=[
            pltpu.VMEM((PAIRS // ccount, 2 * CHUNK // 128, planes, 128), jnp.float32),
            pltpu.VMEM((rows, 512), jnp.float32),
            pltpu.VMEM((2 * (PAIRS // GROUP) * ROWS, 512), jnp.bfloat16),
            pltpu.VMEM((2 * PAIRS, NG), jnp.float32),
        ],
        compiler_params=pltpu.CompilerParams(vmem_limit_bytes=56 * 2**20),
        cost_estimate=pl.CostEstimate(
            flops=rows * FOLD * 512 * 6, bytes_accessed=40 * 2**20, transcendentals=0
        ),
        name="pair_coefficients",
    )(valence, conduction, conduction, *plane_part, *constant, *energies)


def pair_kernel(cols_ref, rows_ref, real_ref, imag_ref, total_ref):
    step = pl.program_id(0)
    values, lines, heights, height, rows = rows_ref.shape
    pieces = []
    for y in range(lines):
        for h in range(heights):
            for v in range(values):
                block = rows_ref[v, y, h].astype(jnp.float32)
                scale = -jnp.exp2(2.0 * block[2 * PAIRS :])
                block = jnp.concatenate(
                    [block[at * 8 : at * 8 + 8] * scale[:, at : at + 1] for at in range(4)]
                )
                turned = jnp.concatenate([block[PAIRS:], -block[:PAIRS]])
                pieces.append(jnp.concatenate([block, turned], axis=1))
    high, low = split(jnp.concatenate(pieces).T)
    both = jnp.concatenate([high, low])
    ch, cl = split(cols_ref[...].astype(jnp.float32))
    part = dot32(both, ch)
    part = part[: 2 * rows] + part[2 * rows :] + dot32(high, cl)

    @pl.when(step == 0)
    def _():
        total_ref[...] = part

    @pl.when(step > 0)
    def _():
        total_ref[...] += part

    @pl.when(step == pl.num_programs(0) - 1)
    def _():
        real_ref[...] = total_ref[:rows]
        imag_ref[...] = total_ref[rows:]


def pair_product(cols, rows):
    count, width = cols.shape
    values, lines, heights, height, short = rows.shape
    each = 4
    depth = count // lines * each
    shape = jax.ShapeDtypeStruct((short, width), jnp.float32)
    out = pl.BlockSpec((short, width), lambda k: (0, 0))
    return pl.pallas_call(
        pair_kernel,
        grid=(lines // each,),
        in_specs=[
            pl.BlockSpec((depth, width), lambda k: (k, 0)),
            pl.BlockSpec((values, each, heights, height, short), lambda k: (0, k, 0, 0, 0)),
        ],
        out_specs=(out, out),
        out_shape=(shape, shape),
        scratch_shapes=[pltpu.VMEM((2 * short, width), jnp.float32)],
        compiler_params=pltpu.CompilerParams(vmem_limit_bytes=48 * 2**20),
        cost_estimate=pl.CostEstimate(
            flops=6 * 2 * short * width * count, bytes_accessed=12 * 2**20, transcendentals=0
        ),
        name="pair_product",
    )(cols, rows)


def sphere_slots(index):
    def quotient(value, divisor):
        exact = (value.astype(jnp.float32) + 0.5) * (1.0 / divisor)
        return jnp.floor(exact).astype(jnp.int32)

    def folded(value):
        return jnp.where(value >= HALF, value - NGRID, value)

    first = quotient(index, PLANE)
    rest = index - first * PLANE
    second = quotient(rest, NGRID)
    third = folded(rest - second * NGRID)
    first, second = folded(first), folded(second)
    sign = jnp.where(third < 0, -1, 1)
    first, second, third = first * sign, second * sign, third * sign
    turn = second + KCUT
    lane = jnp.right_shift(turn, 1) * ELEN + third + jnp.bitwise_and(turn, 1) * 128
    return lane, first + KCUT, sign.astype(jnp.float32)


def pair_gain(valence_ref, conduction_ref, ccount):
    at = lax.broadcasted_iota(jnp.int32, (PAIRS, 1), 0)
    gap = jnp.zeros((PAIRS, 1), jnp.float32)
    for pair in range(PAIRS):
        this = conduction_ref[pair % ccount] - valence_ref[pair // ccount]
        gap = jnp.where(at == pair, this, gap)
    return jnp.sqrt(2.0 / gap * 2048.0**-0.5) * float(NGRID) ** -1.5


def encode(values):
    size = jnp.abs(values.astype(jnp.float32))
    tiny = size < 2.0**-120
    size = jnp.where(tiny, 1.0, size)
    power = jnp.floor(jnp.log2(size))
    mantissa = jnp.round(size * jnp.exp2(7.0 - power)) - 128.0
    power = jnp.where(mantissa > 127.0, power + 1.0, power) - 7.0
    mantissa = jnp.where(mantissa > 127.0, 0.0, mantissa)
    code = power * 256.0 + mantissa + jnp.where(values < 0, 128.0, 0.0)
    return jnp.where(tiny, -32768.0, code).astype(jnp.int16)


def gather_planes(orbitals):
    count, mine = orbitals.shape[:2]
    lines = CHUNK // 128
    steps = FOLD // CHUNK
    codes = encode(orbitals).reshape(count, mine, 2, steps, lines, 128)
    codes = jnp.transpose(codes, (3, 1, 0, 2, 4, 5)).reshape(-1, 128)
    codes = lax.all_gather(codes, "zh", axis=0)
    codes = lax.all_gather(codes, ("y", "x"), axis=0)
    return codes.reshape(32, steps, mine, 2 * count * lines, 128)


def columns_and_rows(cols, rows, steps):
    height, short = rows.shape[1:]
    sent = jnp.concatenate(
        [
            jnp.broadcast_to(rows, (4,) + rows.shape),
            jnp.broadcast_to(steps[:8], (4, 32, 8, short)),
        ],
        axis=2,
    ).reshape(128, height + 8, short)
    sent = lax.all_to_all(sent, VAL + COND, 0, 0, tiled=True)
    line = lax.all_to_all(cols, ("zh",) + VAL, 0, 0, tiled=True)
    cols = lax.all_gather(line, ("y", "x"), axis=0).reshape(-1, cols.shape[-1])
    return cols, sent.reshape(4, 16, 2, height + 8, short)


def per_device(
    valence_orbitals, conduction_orbitals, valence_energy, conduction_energy, sphere_index
):
    coded = pair_coefficients(
        gather_planes(valence_orbitals),
        conduction_orbitals,
        plane_tables(),
        line_tables(),
        sphere_index,
        (valence_energy, conduction_energy),
    )
    return pair_product(*columns_and_rows(*coded))


def solution(mesh):
    names = ("zl", "core", "y", "x", "zh")
    fine = Mesh(mesh.devices.reshape(2, 2, 4, 4, 2), names)
    placed = (P(VAL, COND, None), P(COND, None, None), P(VAL), P(COND), P())
    return jax.shard_map(
        per_device,
        mesh=fine,
        in_specs=placed,
        out_specs=(P(COND, VAL), P(COND, VAL)),
        check_vma=False,
    )
```

```python
import math

import jax
import jax.numpy as jnp
import numpy as np
from jax import lax
from jax.experimental import pallas as pl
from jax.experimental.pallas import tpu as pltpu
from jax.sharding import Mesh, PartitionSpec as P

NGRID = 96
KCUT = 10
NG = 4096
SIDE = 2 * KCUT + 1
HALF = NGRID // 2
PLANE = NGRID * NGRID
FOLD = PLANE // 2
ELEN = KCUT + 1
CHUNK = 512
PAIRS = 16
GROUP = 8
ROWS = 176
CODES = 32767.0
LOG2 = math.log(2.0)
VAL = ("zl", "core")
COND = ("y", "x", "zh")


def split_np(table):
    high = table.astype(jnp.bfloat16)
    low = (table - high.astype(np.float64)).astype(jnp.bfloat16)
    return high, low


def plane_tables():
    phase_y = np.arange(HALF)[:, None, None, None]
    phase_z = np.arange(NGRID)[None, :, None, None]
    zed = np.arange(ELEN)[None, None, None, :]
    blocks = []
    for first in (-KCUT, -KCUT + 1):
        yed = np.arange(first, KCUT + 1, 2)[None, None, :, None]
        angle = (yed * phase_y + zed * phase_z) % NGRID * (2.0 * math.pi / NGRID)
        angle = angle.reshape(FOLD, -1)
        table = np.zeros((FOLD, 256))
        table[:, : angle.shape[1]] = np.cos(angle)
        table[:, 128 : 128 + angle.shape[1]] = -np.sin(angle)
        blocks.append(table)
    even_high, even_low = split_np(blocks[0])
    odd_high, odd_low = split_np(blocks[1])
    return even_high, even_low, odd_high, odd_low


def line_tables():
    freq = np.arange(-KCUT, KCUT + 1)[:, None]
    angle = freq * np.arange(NGRID)[None, :] % NGRID * (2.0 * math.pi / NGRID)
    parts = np.stack([np.cos(angle), np.sin(angle)])
    eye = np.eye(GROUP)
    table = np.einsum("sax,pq->sapqx", parts, eye)
    return split_np(table.reshape(2 * SIDE * GROUP, GROUP * NGRID))


def dot32(left, right):
    return lax.dot_general(
        left, right, (((1,), (0,)), ((), ())), preferred_element_type=jnp.float32
    )


def split(value):
    high = value.astype(jnp.bfloat16)
    low = (value - high.astype(jnp.float32)).astype(jnp.bfloat16)
    return high, low


def decode(code):
    code = code.astype(jnp.int32)
    scale = jnp.exp2(jnp.right_shift(code, 8).astype(jnp.float32))
    low = jnp.bitwise_and(code, 255).astype(jnp.float32)
    return jnp.where(low < 128.0, low + 128.0, -low) * scale


def add_planes(v_ref, c0_ref, c1_ref, eh_ref, el_ref, oh_ref, ol_ref, value_ref, plane_ref):
    vcount, each, planes = value_ref.shape[:3]
    values = decode(v_ref[...]).reshape(planes, vcount * each, 128)
    for v in range(vcount):
        value_ref[v] = jnp.swapaxes(values[:, v * each : (v + 1) * each], 0, 1)
    ccount = c0_ref.shape[0]
    group, each = 4, 16
    lines = CHUNK // 128
    rows = group * planes
    for c in range(0, ccount, group):
        for v in range(vcount):
            parts = [[], []], [[], []]
            for band in range(c, c + group):
                for first in range(0, planes, each):
                    here = slice(first, first + each)
                    d0, d1 = (
                        jnp.concatenate(
                            [value_ref[v, half * lines + r, here] for r in range(lines)], axis=1
                        )
                        * c_ref[band, here].astype(jnp.float32)
                        for half, c_ref in enumerate((c0_ref, c1_ref))
                    )
                    for which, value in enumerate((d0 + d1, d0 - d1)):
                        for part, value in zip(parts[which], split(value)):
                            part.append(value)
            at = (v * ccount + c) * planes
            for which, (highs, lows) in enumerate(parts):
                th = (eh_ref, oh_ref)[which][...]
                tl = (el_ref, ol_ref)[which][...]
                both = dot32(jnp.concatenate(highs + lows), th)
                part = both[:rows] + both[rows:] + dot32(jnp.concatenate(highs), tl)
                plane_ref[at : at + rows, which * 256 : which * 256 + 256] += part


def finish_pairs(
    plane_ref, th_ref, tl_ref, index_ref, valence_ref, conduction_ref,
    cols_ref, rows_ref, fold_ref, coef_ref,
):
    th, tl = th_ref[...], tl_ref[...]
    used = SIDE * GROUP
    groups = PAIRS // GROUP
    for group in range(groups):
        depth = GROUP * NGRID
        high, low = split(plane_ref[group * depth : (group + 1) * depth])
        both = dot32(th, high) + dot32(th, low) + dot32(tl, high)
        cosine, sine = both[:used], both[used:]
        for par in range(2):
            at = par * 256
            real = cosine[:, at : at + 128] + sine[:, at + 128 : at + 256]
            imag = cosine[:, at + 128 : at + 256] - sine[:, at : at + 128]
            for part, value in enumerate((real, imag)):
                first = (part * groups + group) * ROWS
                value = jnp.concatenate([value, jnp.zeros((ROWS - used, 128), jnp.float32)])
                high_part, low_part = split(value)
                fold_ref[first : first + ROWS, par * 128 : par * 128 + 128] = high_part
                fold_ref[first : first + ROWS, 256 + par * 128 : 384 + par * 128] = low_part
    width = 512
    gain = pair_gain(valence_ref, conduction_ref, conduction_ref.shape[0])

    def pick(tile, largest):
        cols = slice(tile * width, (tile + 1) * width)
        lane, freq, sign = sphere_slots(index_ref[:, cols])
        onehot = lax.broadcasted_iota(jnp.int32, (256, width), 0) == lane
        onehot = onehot.astype(jnp.float32).astype(jnp.bfloat16)
        picked = dot32(fold_ref[...], jnp.concatenate([onehot, onehot]))
        totals = [jnp.zeros((GROUP, width), jnp.float32)] * (2 * groups)
        for a in range(SIDE):
            here = freq == a
            for at in range(2 * groups):
                first = at * ROWS + a * GROUP
                totals[at] = jnp.where(here, picked[first : first + GROUP], totals[at])
        for part in range(2):
            total = jnp.concatenate(totals[part * groups : (part + 1) * groups]) * gain
            if part == 1:
                total = total * sign
            coef_ref[part * PAIRS : (part + 1) * PAIRS, cols] = total
            largest = jnp.maximum(largest, jnp.max(jnp.abs(total), axis=1, keepdims=True))
        return largest

    largest = jnp.zeros((PAIRS, 1), jnp.float32)
    for tile in range(NG // width):
        largest = pick(tile, largest)
    usable = largest > 1e-30
    step = jnp.ceil(jnp.log(jnp.where(usable, largest, 1.0) * (1.0 / CODES)) * (1.0 / LOG2))
    lane = lax.broadcasted_iota(jnp.int32, (8, 128), 1)
    powers = jnp.where(lane % 2 == 0, step[:8], step[8:]).astype(jnp.int32)
    inverse = jnp.where(usable, jnp.exp2(-step), 0.0)
    inverse = jnp.concatenate([inverse, inverse])
    each = cols_ref.shape[0] // 2
    for owner in range(each):
        blocks = []
        for block in range(owner * 8, owner * 8 + 8):
            codes = jnp.round(coef_ref[:, block * 128 : (block + 1) * 128] * inverse)
            codes = jnp.clip(codes, -CODES, CODES).astype(jnp.int32)
            for copy in range(0, rows_ref.shape[0], 32):
                rows_ref[copy + block] = codes.astype(jnp.int16)
            blocks.append(codes)
        message = jnp.concatenate(blocks + [powers]).astype(jnp.int16)
        cols_ref[owner] = message
        cols_ref[each + owner] = message


def coefficient_kernel(*refs):
    streamed, constant = refs[:7], refs[7:12]
    outputs = refs[12:14]
    value_ref, plane_ref, fold_ref, coef_ref = refs[14:]

    @pl.when(pl.program_id(0) == 0)
    def _():
        plane_ref[...] = jnp.zeros_like(plane_ref)

    add_planes(*streamed, value_ref, plane_ref)

    @pl.when(pl.program_id(0) == pl.num_programs(0) - 1)
    def _():
        finish_pairs(plane_ref, *constant, *outputs, fold_ref, coef_ref)


def pair_coefficients(valence, conduction, plane_part, line_part, index, energies):
    owners, steps, mine, lines, _ = valence.shape
    planes = owners * mine
    ccount = conduction.shape[0]
    rows = PAIRS * planes
    vspec = pl.BlockSpec((owners, 1, mine, lines, 128), lambda k: (0, k, 0, 0, 0))
    cspec = lambda off: pl.BlockSpec((ccount, planes, CHUNK), lambda k: (0, 0, k + off))
    tspec = pl.BlockSpec((CHUNK, 256), lambda k: (k, 0))
    whole = lambda shape: pl.BlockSpec(shape, lambda k: (0,) * len(shape))
    constant = [*line_part, index.reshape(1, -1)]
    scalar = pl.BlockSpec(memory_space=pltpu.SMEM)
    shapes = ((8, 8 * 2 * PAIRS + 8, 128), (128, 2 * PAIRS, 128))
    return pl.pallas_call(
        coefficient_kernel,
        grid=(steps,),
        in_specs=[vspec, cspec(0), cspec(steps)]
        + [tspec] * 4
        + [whole(value.shape) for value in constant]
        + [scalar, scalar],
        out_specs=tuple(whole(shape) for shape in shapes),
        out_shape=tuple(jax.ShapeDtypeStruct(shape, jnp.int16) for shape in shapes),
        scratch_shapes=[
            pltpu.VMEM((PAIRS // ccount, 2 * CHUNK // 128, planes, 128), jnp.float32),
            pltpu.VMEM((rows, 512), jnp.float32),
            pltpu.VMEM((2 * (PAIRS // GROUP) * ROWS, 512), jnp.bfloat16),
            pltpu.VMEM((2 * PAIRS, NG), jnp.float32),
        ],
        compiler_params=pltpu.CompilerParams(vmem_limit_bytes=56 * 2**20),
        cost_estimate=pl.CostEstimate(
            flops=rows * FOLD * 512 * 6, bytes_accessed=40 * 2**20, transcendentals=0
        ),
        name="pair_coefficients",
    )(valence, conduction, conduction, *plane_part, *constant, *energies)


def pair_kernel(cols_ref, rows_ref, real_ref, imag_ref, total_ref):
    step = pl.program_id(0)
    values, lines, heights, height, rows = rows_ref.shape
    blocks = total_ref.shape[1] // 128
    row_pieces, col_pieces = [], []
    for y in range(lines):
        for h in range(heights):
            for v in range(values):
                codes = cols_ref[y, h * values + v].astype(jnp.float32)
                col_pieces.append(
                    jnp.concatenate(
                        [codes[at * height : (at + 1) * height] for at in range(blocks)], axis=1
                    )
                )
                scale = -jnp.exp2(2.0 * codes[blocks * height :])
                block = rows_ref[v, y, h].astype(jnp.float32)
                block = jnp.concatenate(
                    [block[at * 8 : at * 8 + 8] * scale[:, at : at + 1] for at in range(height // 8)]
                )
                turned = jnp.concatenate([block[PAIRS:], -block[:PAIRS]])
                row_pieces.append(jnp.concatenate([block, turned], axis=1))
    high, low = split(jnp.concatenate(row_pieces).T)
    both = jnp.concatenate([high, low])
    ch, cl = split(jnp.concatenate(col_pieces))
    part = dot32(both, ch)
    part = part[: 2 * rows] + part[2 * rows :] + dot32(high, cl)

    @pl.when(step == 0)
    def _():
        total_ref[...] = part

    @pl.when(step > 0)
    def _():
        total_ref[...] += part

    @pl.when(step == pl.num_programs(0) - 1)
    def _():
        real_ref[...] = total_ref[:rows]
        imag_ref[...] = total_ref[rows:]


def pair_product(cols, rows):
    values, lines, heights, height, short = rows.shape
    width = cols.shape[2] // height * 128
    count = lines * heights * values * height
    each = 4
    shape = jax.ShapeDtypeStruct((short, width), jnp.float32)
    out = pl.BlockSpec((short, width), lambda k: (0, 0))
    return pl.pallas_call(
        pair_kernel,
        grid=(lines // each,),
        in_specs=[
            pl.BlockSpec((each,) + cols.shape[1:], lambda k: (k, 0, 0, 0)),
            pl.BlockSpec((values, each, heights, height, short), lambda k: (0, k, 0, 0, 0)),
        ],
        out_specs=(out, out),
        out_shape=(shape, shape),
        scratch_shapes=[pltpu.VMEM((2 * short, width), jnp.float32)],
        compiler_params=pltpu.CompilerParams(vmem_limit_bytes=48 * 2**20),
        cost_estimate=pl.CostEstimate(
            flops=6 * 2 * short * width * count, bytes_accessed=12 * 2**20, transcendentals=0
        ),
        name="pair_product",
    )(cols, rows)


def sphere_slots(index):
    def quotient(value, divisor):
        exact = (value.astype(jnp.float32) + 0.5) * (1.0 / divisor)
        return jnp.floor(exact).astype(jnp.int32)

    def folded(value):
        return jnp.where(value >= HALF, value - NGRID, value)

    first = quotient(index, PLANE)
    rest = index - first * PLANE
    second = quotient(rest, NGRID)
    third = folded(rest - second * NGRID)
    first, second = folded(first), folded(second)
    sign = jnp.where(third < 0, -1, 1)
    first, second, third = first * sign, second * sign, third * sign
    turn = second + KCUT
    lane = jnp.right_shift(turn, 1) * ELEN + third + jnp.bitwise_and(turn, 1) * 128
    return lane, first + KCUT, sign.astype(jnp.float32)


def pair_gain(valence_ref, conduction_ref, ccount):
    at = lax.broadcasted_iota(jnp.int32, (PAIRS, 1), 0)
    gap = jnp.zeros((PAIRS, 1), jnp.float32)
    for pair in range(PAIRS):
        this = conduction_ref[pair % ccount] - valence_ref[pair // ccount]
        gap = jnp.where(at == pair, this, gap)
    return jnp.sqrt(2.0 / gap * 2048.0**-0.5) * float(NGRID) ** -1.5


def encode(values):
    size = jnp.abs(values.astype(jnp.float32))
    tiny = size < 2.0**-120
    size = jnp.where(tiny, 1.0, size)
    power = jnp.floor(jnp.log2(size))
    mantissa = jnp.round(size * jnp.exp2(7.0 - power)) - 128.0
    power = jnp.where(mantissa > 127.0, power + 1.0, power) - 7.0
    mantissa = jnp.where(mantissa > 127.0, 0.0, mantissa)
    code = power * 256.0 + mantissa + jnp.where(values < 0, 128.0, 0.0)
    return jnp.where(tiny, -32768.0, code).astype(jnp.int16)


def gather_planes(orbitals):
    count, mine = orbitals.shape[:2]
    lines = CHUNK // 128
    steps = FOLD // CHUNK
    codes = encode(orbitals).reshape(count, mine, 2, steps, lines, 128)
    codes = jnp.transpose(codes, (3, 1, 0, 2, 4, 5)).reshape(-1, 128)
    codes = lax.all_gather(codes, "zh", axis=0)
    codes = lax.all_gather(codes, ("y", "x"), axis=0)
    return codes.reshape(32, steps, mine, 2 * count * lines, 128)


def columns_and_rows(cols, rows):
    sent = lax.all_to_all(rows, VAL + COND, 0, 0, tiled=True)
    line = lax.all_to_all(cols, ("zh",) + VAL, 0, 0, tiled=True)
    return lax.all_gather(line, ("y", "x"), axis=0), sent.reshape((4, 16, 2) + rows.shape[1:])


def per_device(
    valence_orbitals, conduction_orbitals, valence_energy, conduction_energy, sphere_index
):
    coded = pair_coefficients(
        gather_planes(valence_orbitals),
        conduction_orbitals,
        plane_tables(),
        line_tables(),
        sphere_index,
        (valence_energy, conduction_energy),
    )
    return pair_product(*columns_and_rows(*coded))


def solution(mesh):
    names = ("zl", "core", "y", "x", "zh")
    fine = Mesh(mesh.devices.reshape(2, 2, 4, 4, 2), names)
    placed = (P(VAL, COND, None), P(COND, None, None), P(VAL), P(COND), P())
    return jax.shard_map(
        per_device,
        mesh=fine,
        in_specs=placed,
        out_specs=(P(COND, VAL), P(COND, VAL)),
        check_vma=False,
    )
```

```python
import math

import jax
import jax.numpy as jnp
import numpy as np
from jax import lax
from jax.experimental import pallas as pl
from jax.experimental.pallas import tpu as pltpu
from jax.sharding import Mesh, PartitionSpec as P

NGRID = 96
KCUT = 10
NG = 4096
SIDE = 2 * KCUT + 1
HALF = NGRID // 2
PLANE = NGRID * NGRID
FOLD = PLANE // 2
ELEN = KCUT + 1
CHUNK = 512
PAIRS = 16
GROUP = 8
ROWS = 176
CODES = 32767.0
LIFT = 80.0
LOG2 = math.log(2.0)
VAL = ("zl", "core")
COND = ("y", "x", "zh")


def split_np(table):
    high = table.astype(jnp.bfloat16)
    low = (table - high.astype(np.float64)).astype(jnp.bfloat16)
    return high, low


def plane_tables():
    phase_y = np.arange(HALF)[:, None, None, None]
    phase_z = np.arange(NGRID)[None, :, None, None]
    zed = np.arange(ELEN)[None, None, None, :]
    blocks = []
    for first in (-KCUT, -KCUT + 1):
        yed = np.arange(first, KCUT + 1, 2)[None, None, :, None]
        angle = (yed * phase_y + zed * phase_z) % NGRID * (2.0 * math.pi / NGRID)
        angle = angle.reshape(FOLD, -1)
        table = np.zeros((FOLD, 256))
        table[:, : angle.shape[1]] = np.cos(angle)
        table[:, 128 : 128 + angle.shape[1]] = -np.sin(angle)
        blocks.append(table)
    even_high, even_low = split_np(blocks[0])
    odd_high, odd_low = split_np(blocks[1])
    return even_high, even_low, odd_high, odd_low


def line_tables():
    freq = np.arange(-KCUT, KCUT + 1)[:, None]
    angle = freq * np.arange(NGRID)[None, :] % NGRID * (2.0 * math.pi / NGRID)
    parts = np.stack([np.cos(angle), np.sin(angle)])
    eye = np.eye(GROUP)
    table = np.einsum("sax,pq->sapqx", parts, eye)
    return split_np(table.reshape(2 * SIDE * GROUP, GROUP * NGRID))


def dot32(left, right):
    return lax.dot_general(
        left, right, (((1,), (0,)), ((), ())), preferred_element_type=jnp.float32
    )


def split(value):
    high = value.astype(jnp.bfloat16)
    low = (value - high.astype(jnp.float32)).astype(jnp.bfloat16)
    return high, low


def decode(code):
    code = code.astype(jnp.int32)
    scale = jnp.exp2(jnp.right_shift(code, 8).astype(jnp.float32))
    low = jnp.bitwise_and(code, 255).astype(jnp.float32)
    return jnp.where(low < 128.0, low + 128.0, -low) * scale


def add_planes(v_ref, c0_ref, c1_ref, eh_ref, el_ref, oh_ref, ol_ref, value_ref, plane_ref):
    vcount, each, planes = value_ref.shape[:3]
    values = decode(v_ref[...]).reshape(planes, vcount * each, 128)
    for v in range(vcount):
        value_ref[v] = jnp.swapaxes(values[:, v * each : (v + 1) * each], 0, 1)
    ccount = c0_ref.shape[0]
    group, each = 4, 16
    lines = CHUNK // 128
    rows = group * planes
    for c in range(0, ccount, group):
        for v in range(vcount):
            parts = [[], []], [[], []]
            for band in range(c, c + group):
                for first in range(0, planes, each):
                    here = slice(first, first + each)
                    d0, d1 = (
                        jnp.concatenate(
                            [value_ref[v, half * lines + r, here] for r in range(lines)], axis=1
                        )
                        * c_ref[band, here].astype(jnp.float32)
                        for half, c_ref in enumerate((c0_ref, c1_ref))
                    )
                    for which, value in enumerate((d0 + d1, d0 - d1)):
                        for part, value in zip(parts[which], split(value)):
                            part.append(value)
            at = (v * ccount + c) * planes
            for which, (highs, lows) in enumerate(parts):
                th = (eh_ref, oh_ref)[which][...]
                tl = (el_ref, ol_ref)[which][...]
                both = dot32(jnp.concatenate(highs + lows), th)
                part = both[:rows] + both[rows:] + dot32(jnp.concatenate(highs), tl)
                plane_ref[at : at + rows, which * 256 : which * 256 + 256] += part


def finish_pairs(
    plane_ref, th_ref, tl_ref, index_ref, valence_ref, conduction_ref,
    cols_ref, rows_ref, fold_ref, coef_ref,
):
    th, tl = th_ref[...], tl_ref[...]
    used = SIDE * GROUP
    groups = PAIRS // GROUP
    for group in range(groups):
        depth = GROUP * NGRID
        high, low = split(plane_ref[group * depth : (group + 1) * depth])
        both = dot32(th, high) + dot32(th, low) + dot32(tl, high)
        cosine, sine = both[:used], both[used:]
        for par in range(2):
            at = par * 256
            real = cosine[:, at : at + 128] + sine[:, at + 128 : at + 256]
            imag = cosine[:, at + 128 : at + 256] - sine[:, at : at + 128]
            for part, value in enumerate((real, imag)):
                first = (part * groups + group) * ROWS
                value = jnp.concatenate([value, jnp.zeros((ROWS - used, 128), jnp.float32)])
                high_part, low_part = split(value)
                fold_ref[first : first + ROWS, par * 128 : par * 128 + 128] = high_part
                fold_ref[first : first + ROWS, 256 + par * 128 : 384 + par * 128] = low_part
    width = 512
    gain = pair_gain(valence_ref, conduction_ref, conduction_ref.shape[0])

    def pick(tile, largest):
        cols = slice(tile * width, (tile + 1) * width)
        lane, freq, sign = sphere_slots(index_ref[:, cols])
        onehot = lax.broadcasted_iota(jnp.int32, (256, width), 0) == lane
        onehot = onehot.astype(jnp.float32).astype(jnp.bfloat16)
        picked = dot32(fold_ref[...], jnp.concatenate([onehot, onehot]))
        totals = [jnp.zeros((GROUP, width), jnp.float32)] * (2 * groups)
        for a in range(SIDE):
            here = freq == a
            for at in range(2 * groups):
                first = at * ROWS + a * GROUP
                totals[at] = jnp.where(here, picked[first : first + GROUP], totals[at])
        for part in range(2):
            total = jnp.concatenate(totals[part * groups : (part + 1) * groups]) * gain
            if part == 1:
                total = total * sign
            coef_ref[part * PAIRS : (part + 1) * PAIRS, cols] = total
            largest = jnp.maximum(largest, jnp.max(jnp.abs(total), axis=1, keepdims=True))
        return largest

    largest = jnp.zeros((PAIRS, 1), jnp.float32)
    for tile in range(NG // width):
        largest = pick(tile, largest)
    usable = largest > 1e-30
    step = jnp.ceil(jnp.log(jnp.where(usable, largest, 1.0) * (1.0 / CODES)) * (1.0 / LOG2))
    lane = lax.broadcasted_iota(jnp.int32, (8, 128), 1)
    powers = jnp.where(lane % 2 == 0, step[:8], step[8:]).astype(jnp.int32)
    inverse = jnp.where(usable, jnp.exp2(-step), 0.0)
    inverse = jnp.concatenate([inverse, inverse])
    each = cols_ref.shape[0] // 2
    for owner in range(each):
        blocks = []
        for block in range(owner * 8, owner * 8 + 8):
            codes = jnp.round(coef_ref[:, block * 128 : (block + 1) * 128] * inverse)
            codes = jnp.clip(codes, -CODES, CODES).astype(jnp.int32)
            for copy in range(0, rows_ref.shape[0], 32):
                rows_ref[copy + block] = codes.astype(jnp.int16)
            blocks.append(codes)
        message = jnp.concatenate(blocks + [powers]).astype(jnp.int16)
        cols_ref[owner] = message
        cols_ref[each + owner] = message


def coefficient_kernel(*refs):
    streamed, constant = refs[:7], refs[7:12]
    outputs = refs[12:14]
    value_ref, plane_ref, fold_ref, coef_ref = refs[14:]

    @pl.when(pl.program_id(0) == 0)
    def _():
        plane_ref[...] = jnp.zeros_like(plane_ref)

    add_planes(*streamed, value_ref, plane_ref)

    @pl.when(pl.program_id(0) == pl.num_programs(0) - 1)
    def _():
        finish_pairs(plane_ref, *constant, *outputs, fold_ref, coef_ref)


def pair_coefficients(valence, conduction, plane_part, line_part, index, energies):
    owners, steps, mine, lines, _ = valence.shape
    planes = owners * mine
    ccount = conduction.shape[0]
    rows = PAIRS * planes
    vspec = pl.BlockSpec((owners, 1, mine, lines, 128), lambda k: (0, k, 0, 0, 0))
    cspec = lambda off: pl.BlockSpec((ccount, planes, CHUNK), lambda k: (0, 0, k + off))
    tspec = pl.BlockSpec((CHUNK, 256), lambda k: (k, 0))
    whole = lambda shape: pl.BlockSpec(shape, lambda k: (0,) * len(shape))
    constant = [*line_part, index.reshape(1, -1)]
    scalar = pl.BlockSpec(memory_space=pltpu.SMEM)
    shapes = ((8, 8 * 2 * PAIRS + 8, 128), (128, 2 * PAIRS, 128))
    return pl.pallas_call(
        coefficient_kernel,
        grid=(steps,),
        in_specs=[vspec, cspec(0), cspec(steps)]
        + [tspec] * 4
        + [whole(value.shape) for value in constant]
        + [scalar, scalar],
        out_specs=tuple(whole(shape) for shape in shapes),
        out_shape=tuple(jax.ShapeDtypeStruct(shape, jnp.int16) for shape in shapes),
        scratch_shapes=[
            pltpu.VMEM((PAIRS // ccount, 2 * CHUNK // 128, planes, 128), jnp.float32),
            pltpu.VMEM((rows, 512), jnp.float32),
            pltpu.VMEM((2 * (PAIRS // GROUP) * ROWS, 512), jnp.bfloat16),
            pltpu.VMEM((2 * PAIRS, NG), jnp.float32),
        ],
        compiler_params=pltpu.CompilerParams(vmem_limit_bytes=56 * 2**20),
        cost_estimate=pl.CostEstimate(
            flops=rows * FOLD * 512 * 6, bytes_accessed=40 * 2**20, transcendentals=0
        ),
        name="pair_coefficients",
    )(valence, conduction, conduction, *plane_part, *constant, *energies)


def pair_kernel(cols_ref, rows_ref, real_ref, imag_ref, total_ref):
    step = pl.program_id(0)
    values, lines, heights, height, rows = rows_ref.shape
    blocks = total_ref.shape[1] // 128
    row_pieces, col_pieces = [], []
    for y in range(lines):
        for h in range(heights):
            for v in range(values):
                codes = cols_ref[y, h * values + v].astype(jnp.float32)
                col_pieces.append(
                    jnp.concatenate(
                        [codes[at * height : (at + 1) * height] for at in range(blocks)], axis=1
                    )
                )
                scale = -jnp.exp2(2.0 * codes[blocks * height :] + LIFT)
                block = rows_ref[v, y, h].astype(jnp.float32)
                block = jnp.concatenate(
                    [block[at * 8 : at * 8 + 8] * scale[:, at : at + 1] for at in range(height // 8)]
                )
                turned = jnp.concatenate([block[PAIRS:], -block[:PAIRS]])
                row_pieces.append(jnp.concatenate([block, turned], axis=1))
    high, low = split(jnp.concatenate(row_pieces).T)
    both = jnp.concatenate([high, low])
    ch, cl = split(jnp.concatenate(col_pieces))
    part = dot32(both, ch)
    part = part[: 2 * rows] + part[2 * rows :] + dot32(high, cl)

    @pl.when(step == 0)
    def _():
        total_ref[...] = part

    @pl.when(step > 0)
    def _():
        total_ref[...] += part

    @pl.when(step == pl.num_programs(0) - 1)
    def _():
        real_ref[...] = total_ref[:rows] * 2.0**-LIFT
        imag_ref[...] = total_ref[rows:] * 2.0**-LIFT


def pair_product(cols, rows):
    values, lines, heights, height, short = rows.shape
    width = cols.shape[2] // height * 128
    count = lines * heights * values * height
    each = 4
    shape = jax.ShapeDtypeStruct((short, width), jnp.float32)
    out = pl.BlockSpec((short, width), lambda k: (0, 0))
    return pl.pallas_call(
        pair_kernel,
        grid=(lines // each,),
        in_specs=[
            pl.BlockSpec((each,) + cols.shape[1:], lambda k: (k, 0, 0, 0)),
            pl.BlockSpec((values, each, heights, height, short), lambda k: (0, k, 0, 0, 0)),
        ],
        out_specs=(out, out),
        out_shape=(shape, shape),
        scratch_shapes=[pltpu.VMEM((2 * short, width), jnp.float32)],
        compiler_params=pltpu.CompilerParams(vmem_limit_bytes=48 * 2**20),
        cost_estimate=pl.CostEstimate(
            flops=6 * 2 * short * width * count, bytes_accessed=12 * 2**20, transcendentals=0
        ),
        name="pair_product",
    )(cols, rows)


def sphere_slots(index):
    def quotient(value, divisor):
        exact = (value.astype(jnp.float32) + 0.5) * (1.0 / divisor)
        return jnp.floor(exact).astype(jnp.int32)

    def folded(value):
        return jnp.where(value >= HALF, value - NGRID, value)

    first = quotient(index, PLANE)
    rest = index - first * PLANE
    second = quotient(rest, NGRID)
    third = folded(rest - second * NGRID)
    first, second = folded(first), folded(second)
    sign = jnp.where(third < 0, -1, 1)
    first, second, third = first * sign, second * sign, third * sign
    turn = second + KCUT
    lane = jnp.right_shift(turn, 1) * ELEN + third + jnp.bitwise_and(turn, 1) * 128
    return lane, first + KCUT, sign.astype(jnp.float32)


def pair_gain(valence_ref, conduction_ref, ccount):
    at = lax.broadcasted_iota(jnp.int32, (PAIRS, 1), 0)
    gap = jnp.zeros((PAIRS, 1), jnp.float32)
    for pair in range(PAIRS):
        this = conduction_ref[pair % ccount] - valence_ref[pair // ccount]
        gap = jnp.where(at == pair, this, gap)
    return jnp.sqrt(2.0 / gap * 2048.0**-0.5) * float(NGRID) ** -1.5


def encode(values):
    size = jnp.abs(values.astype(jnp.float32))
    tiny = size < 2.0**-120
    size = jnp.where(tiny, 1.0, size)
    power = jnp.floor(jnp.log2(size))
    mantissa = jnp.round(size * jnp.exp2(7.0 - power)) - 128.0
    power = jnp.where(mantissa > 127.0, power + 1.0, power) - 7.0
    mantissa = jnp.where(mantissa > 127.0, 0.0, mantissa)
    code = power * 256.0 + mantissa + jnp.where(values < 0, 128.0, 0.0)
    return jnp.where(tiny, -32768.0, code).astype(jnp.int16)


def gather_planes(orbitals):
    count, mine = orbitals.shape[:2]
    lines = CHUNK // 128
    steps = FOLD // CHUNK
    codes = encode(orbitals).reshape(count, mine, 2, steps, lines, 128)
    codes = jnp.transpose(codes, (3, 1, 0, 2, 4, 5)).reshape(-1, 128)
    codes = lax.all_gather(codes, "zh", axis=0)
    codes = lax.all_gather(codes, ("y", "x"), axis=0)
    return codes.reshape(32, steps, mine, 2 * count * lines, 128)


def columns_and_rows(cols, rows):
    sent = lax.all_to_all(rows, VAL + COND, 0, 0, tiled=True)
    line = lax.all_to_all(cols, ("zh",) + VAL, 0, 0, tiled=True)
    return lax.all_gather(line, ("y", "x"), axis=0), sent.reshape((4, 16, 2) + rows.shape[1:])


def per_device(
    valence_orbitals, conduction_orbitals, valence_energy, conduction_energy, sphere_index
):
    coded = pair_coefficients(
        gather_planes(valence_orbitals),
        conduction_orbitals,
        plane_tables(),
        line_tables(),
        sphere_index,
        (valence_energy, conduction_energy),
    )
    return pair_product(*columns_and_rows(*coded))


def solution(mesh):
    names = ("zl", "core", "y", "x", "zh")
    fine = Mesh(mesh.devices.reshape(2, 2, 4, 4, 2), names)
    placed = (P(VAL, COND, None), P(COND, None, None), P(VAL), P(COND), P())
    return jax.shard_map(
        per_device,
        mesh=fine,
        in_specs=placed,
        out_specs=(P(COND, VAL), P(COND, VAL)),
        check_vma=False,
    )
```

```python
import math

import jax
import jax.numpy as jnp
import numpy as np
from jax import lax
from jax.experimental import pallas as pl
from jax.experimental.pallas import tpu as pltpu
from jax.sharding import Mesh, PartitionSpec as P

NGRID = 96
KCUT = 10
NG = 4096
SIDE = 2 * KCUT + 1
HALF = NGRID // 2
PLANE = NGRID * NGRID
FOLD = PLANE // 2
ELEN = KCUT + 1
CHUNK = 512
PAIRS = 16
GROUP = 8
ROWS = 176
CODES = 32767.0
LIFT = 80.0
LOG2 = math.log(2.0)
VAL = ("zl", "core")
COND = ("y", "x", "zh")


def split_np(table):
    high = table.astype(jnp.bfloat16)
    low = (table - high.astype(np.float64)).astype(jnp.bfloat16)
    return high, low


def plane_tables():
    phase_y = np.arange(HALF)[:, None, None, None]
    phase_z = np.arange(NGRID)[None, :, None, None]
    zed = np.arange(ELEN)[None, None, None, :]
    blocks = []
    for first in (-KCUT, -KCUT + 1):
        yed = np.arange(first, KCUT + 1, 2)[None, None, :, None]
        angle = (yed * phase_y + zed * phase_z) % NGRID * (2.0 * math.pi / NGRID)
        angle = angle.reshape(FOLD, -1)
        table = np.zeros((FOLD, 256))
        table[:, : angle.shape[1]] = np.cos(angle)
        table[:, 128 : 128 + angle.shape[1]] = -np.sin(angle)
        blocks.append(table)
    even_high, even_low = split_np(blocks[0])
    odd_high, odd_low = split_np(blocks[1])
    return even_high, even_low, odd_high, odd_low


def line_tables():
    freq = np.arange(-KCUT, KCUT + 1)[:, None]
    angle = freq * np.arange(NGRID)[None, :] % NGRID * (2.0 * math.pi / NGRID)
    parts = np.stack([np.cos(angle), np.sin(angle)])
    eye = np.eye(GROUP)
    table = np.einsum("sax,pq->sapqx", parts, eye)
    return split_np(table.reshape(2 * SIDE * GROUP, GROUP * NGRID))


def dot32(left, right):
    return lax.dot_general(
        left, right, (((1,), (0,)), ((), ())), preferred_element_type=jnp.float32
    )


def split(value):
    high = value.astype(jnp.bfloat16)
    low = (value - high.astype(jnp.float32)).astype(jnp.bfloat16)
    return high, low


def decode(code):
    code = code.astype(jnp.int32)
    scale = jnp.exp2(jnp.right_shift(code, 8).astype(jnp.float32))
    low = jnp.bitwise_and(code, 255).astype(jnp.float32)
    return jnp.where(low < 128.0, low + 128.0, -low) * scale


def add_planes(v_ref, c0_ref, c1_ref, eh_ref, el_ref, oh_ref, ol_ref, value_ref, plane_ref):
    vcount, each, planes = value_ref.shape[:3]
    values = decode(v_ref[...]).reshape(planes, vcount * each, 128)
    for v in range(vcount):
        value_ref[v] = jnp.swapaxes(values[:, v * each : (v + 1) * each], 0, 1)
    ccount = c0_ref.shape[0]
    group, each = 4, 16
    lines = CHUNK // 128
    rows = group * planes
    for c in range(0, ccount, group):
        for v in range(vcount):
            parts = [[], []], [[], []]
            for band in range(c, c + group):
                for first in range(0, planes, each):
                    here = slice(first, first + each)
                    d0, d1 = (
                        jnp.concatenate(
                            [value_ref[v, half * lines + r, here] for r in range(lines)], axis=1
                        )
                        * c_ref[band, here].astype(jnp.float32)
                        for half, c_ref in enumerate((c0_ref, c1_ref))
                    )
                    for which, value in enumerate((d0 + d1, d0 - d1)):
                        for part, value in zip(parts[which], split(value)):
                            part.append(value)
            at = (v * ccount + c) * planes
            for which, (highs, lows) in enumerate(parts):
                th = (eh_ref, oh_ref)[which][...]
                tl = (el_ref, ol_ref)[which][...]
                both = dot32(jnp.concatenate(highs + lows), th)
                part = both[:rows] + both[rows:] + dot32(jnp.concatenate(highs), tl)
                plane_ref[at : at + rows, which * 256 : which * 256 + 256] += part


def finish_pairs(
    plane_ref, th_ref, tl_ref, index_ref, valence_ref, conduction_ref,
    cols_ref, rows_ref, fold_ref, coef_ref,
):
    th = th_ref[...]
    tables = jnp.concatenate([th, tl_ref[...]])
    used = SIDE * GROUP
    groups = PAIRS // GROUP
    for group in range(groups):
        depth = GROUP * NGRID
        high, low = split(plane_ref[group * depth : (group + 1) * depth])
        first_sums = dot32(tables, high)
        both = first_sums[: 2 * used] + first_sums[2 * used :] + dot32(th, low)
        cosine, sine = both[:used], both[used:]
        for par in range(2):
            at = par * 256
            real = cosine[:, at : at + 128] + sine[:, at + 128 : at + 256]
            imag = cosine[:, at + 128 : at + 256] - sine[:, at : at + 128]
            for part, value in enumerate((real, imag)):
                first = (part * groups + group) * ROWS
                value = jnp.concatenate([value, jnp.zeros((ROWS - used, 128), jnp.float32)])
                high_part, low_part = split(value)
                fold_ref[first : first + ROWS, par * 128 : par * 128 + 128] = high_part
                fold_ref[first : first + ROWS, 256 + par * 128 : 384 + par * 128] = low_part
    width = 512
    gain = pair_gain(valence_ref, conduction_ref, conduction_ref.shape[0])

    def pick(tile, largest):
        cols = slice(tile * width, (tile + 1) * width)
        lane, freq, sign = sphere_slots(index_ref[:, cols])
        onehot = lax.broadcasted_iota(jnp.int32, (256, width), 0) == lane
        onehot = onehot.astype(jnp.float32).astype(jnp.bfloat16)
        picked = dot32(fold_ref[...], jnp.concatenate([onehot, onehot]))
        totals = [jnp.zeros((GROUP, width), jnp.float32)] * (2 * groups)
        for a in range(SIDE):
            here = freq == a
            for at in range(2 * groups):
                first = at * ROWS + a * GROUP
                totals[at] = jnp.where(here, picked[first : first + GROUP], totals[at])
        for part in range(2):
            total = jnp.concatenate(totals[part * groups : (part + 1) * groups]) * gain
            if part == 1:
                total = total * sign
            coef_ref[part * PAIRS : (part + 1) * PAIRS, cols] = total
            largest = jnp.maximum(largest, jnp.max(jnp.abs(total), axis=1, keepdims=True))
        return largest

    largest = jnp.zeros((PAIRS, 1), jnp.float32)
    for tile in range(NG // width):
        largest = pick(tile, largest)
    usable = largest > 1e-30
    step = jnp.ceil(jnp.log(jnp.where(usable, largest, 1.0) * (1.0 / CODES)) * (1.0 / LOG2))
    lane = lax.broadcasted_iota(jnp.int32, (8, 128), 1)
    powers = jnp.where(lane % 2 == 0, step[:8], step[8:]).astype(jnp.int32)
    inverse = jnp.where(usable, jnp.exp2(-step), 0.0)
    inverse = jnp.concatenate([inverse, inverse])
    each = cols_ref.shape[0] // 2
    for owner in range(each):
        blocks = []
        for block in range(owner * 8, owner * 8 + 8):
            codes = jnp.round(coef_ref[:, block * 128 : (block + 1) * 128] * inverse)
            codes = jnp.clip(codes, -CODES, CODES).astype(jnp.int32)
            for copy in range(0, rows_ref.shape[0], 32):
                rows_ref[copy + block] = codes.astype(jnp.int16)
            blocks.append(codes)
        message = jnp.concatenate(blocks + [powers]).astype(jnp.int16)
        cols_ref[owner] = message
        cols_ref[each + owner] = message


def coefficient_kernel(*refs):
    streamed, constant = refs[:7], refs[7:12]
    outputs = refs[12:14]
    value_ref, plane_ref, fold_ref, coef_ref = refs[14:]

    @pl.when(pl.program_id(0) == 0)
    def _():
        plane_ref[...] = jnp.zeros_like(plane_ref)

    add_planes(*streamed, value_ref, plane_ref)

    @pl.when(pl.program_id(0) == pl.num_programs(0) - 1)
    def _():
        finish_pairs(plane_ref, *constant, *outputs, fold_ref, coef_ref)


def pair_coefficients(valence, conduction, plane_part, line_part, index, energies):
    owners, steps, mine, lines, _ = valence.shape
    planes = owners * mine
    ccount = conduction.shape[0]
    rows = PAIRS * planes
    vspec = pl.BlockSpec((owners, 1, mine, lines, 128), lambda k: (0, k, 0, 0, 0))
    cspec = lambda off: pl.BlockSpec((ccount, planes, CHUNK), lambda k: (0, 0, k + off))
    tspec = pl.BlockSpec((CHUNK, 256), lambda k: (k, 0))
    whole = lambda shape: pl.BlockSpec(shape, lambda k: (0,) * len(shape))
    constant = [*line_part, index.reshape(1, -1)]
    scalar = pl.BlockSpec(memory_space=pltpu.SMEM)
    shapes = ((8, 8 * 2 * PAIRS + 8, 128), (128, 2 * PAIRS, 128))
    return pl.pallas_call(
        coefficient_kernel,
        grid=(steps,),
        in_specs=[vspec, cspec(0), cspec(steps)]
        + [tspec] * 4
        + [whole(value.shape) for value in constant]
        + [scalar, scalar],
        out_specs=tuple(whole(shape) for shape in shapes),
        out_shape=tuple(jax.ShapeDtypeStruct(shape, jnp.int16) for shape in shapes),
        scratch_shapes=[
            pltpu.VMEM((PAIRS // ccount, 2 * CHUNK // 128, planes, 128), jnp.float32),
            pltpu.VMEM((rows, 512), jnp.float32),
            pltpu.VMEM((2 * (PAIRS // GROUP) * ROWS, 512), jnp.bfloat16),
            pltpu.VMEM((2 * PAIRS, NG), jnp.float32),
        ],
        compiler_params=pltpu.CompilerParams(vmem_limit_bytes=56 * 2**20),
        cost_estimate=pl.CostEstimate(
            flops=rows * FOLD * 512 * 6, bytes_accessed=40 * 2**20, transcendentals=0
        ),
        name="pair_coefficients",
    )(valence, conduction, conduction, *plane_part, *constant, *energies)


def pair_kernel(cols_ref, rows_ref, real_ref, imag_ref, total_ref):
    step = pl.program_id(0)
    values, lines, heights, height, rows = rows_ref.shape
    blocks = total_ref.shape[1] // 128
    row_pieces, col_pieces = [], []
    for y in range(lines):
        for h in range(heights):
            for v in range(values):
                codes = cols_ref[y, h * values + v].astype(jnp.float32)
                col_pieces.append(
                    jnp.concatenate(
                        [codes[at * height : (at + 1) * height] for at in range(blocks)], axis=1
                    )
                )
                scale = -jnp.exp2(2.0 * codes[blocks * height :] + LIFT)
                block = rows_ref[v, y, h].astype(jnp.float32)
                block = jnp.concatenate(
                    [block[at * 8 : at * 8 + 8] * scale[:, at : at + 1] for at in range(height // 8)]
                )
                turned = jnp.concatenate([block[PAIRS:], -block[:PAIRS]])
                row_pieces.append(jnp.concatenate([block, turned], axis=1))
    high, low = split(jnp.concatenate(row_pieces).T)
    both = jnp.concatenate([high, low])
    ch, cl = split(jnp.concatenate(col_pieces))
    part = dot32(both, ch)
    part = part[: 2 * rows] + part[2 * rows :] + dot32(high, cl)

    @pl.when(step == 0)
    def _():
        total_ref[...] = part

    @pl.when(step > 0)
    def _():
        total_ref[...] += part

    @pl.when(step == pl.num_programs(0) - 1)
    def _():
        real_ref[...] = total_ref[:rows] * 2.0**-LIFT
        imag_ref[...] = total_ref[rows:] * 2.0**-LIFT


def pair_product(cols, rows):
    values, lines, heights, height, short = rows.shape
    width = cols.shape[2] // height * 128
    count = lines * heights * values * height
    each = 4
    shape = jax.ShapeDtypeStruct((short, width), jnp.float32)
    out = pl.BlockSpec((short, width), lambda k: (0, 0))
    return pl.pallas_call(
        pair_kernel,
        grid=(lines // each,),
        in_specs=[
            pl.BlockSpec((each,) + cols.shape[1:], lambda k: (k, 0, 0, 0)),
            pl.BlockSpec((values, each, heights, height, short), lambda k: (0, k, 0, 0, 0)),
        ],
        out_specs=(out, out),
        out_shape=(shape, shape),
        scratch_shapes=[pltpu.VMEM((2 * short, width), jnp.float32)],
        compiler_params=pltpu.CompilerParams(vmem_limit_bytes=48 * 2**20),
        cost_estimate=pl.CostEstimate(
            flops=6 * 2 * short * width * count, bytes_accessed=12 * 2**20, transcendentals=0
        ),
        name="pair_product",
    )(cols, rows)


def sphere_slots(index):
    def quotient(value, divisor):
        exact = (value.astype(jnp.float32) + 0.5) * (1.0 / divisor)
        return jnp.floor(exact).astype(jnp.int32)

    def folded(value):
        return jnp.where(value >= HALF, value - NGRID, value)

    first = quotient(index, PLANE)
    rest = index - first * PLANE
    second = quotient(rest, NGRID)
    third = folded(rest - second * NGRID)
    first, second = folded(first), folded(second)
    sign = jnp.where(third < 0, -1, 1)
    first, second, third = first * sign, second * sign, third * sign
    turn = second + KCUT
    lane = jnp.right_shift(turn, 1) * ELEN + third + jnp.bitwise_and(turn, 1) * 128
    return lane, first + KCUT, sign.astype(jnp.float32)


def pair_gain(valence_ref, conduction_ref, ccount):
    at = lax.broadcasted_iota(jnp.int32, (PAIRS, 1), 0)
    gap = jnp.zeros((PAIRS, 1), jnp.float32)
    for pair in range(PAIRS):
        this = conduction_ref[pair % ccount] - valence_ref[pair // ccount]
        gap = jnp.where(at == pair, this, gap)
    return jnp.sqrt(2.0 / gap * 2048.0**-0.5) * float(NGRID) ** -1.5


def encode(values):
    size = jnp.abs(values.astype(jnp.float32))
    tiny = size < 2.0**-120
    size = jnp.where(tiny, 1.0, size)
    power = jnp.floor(jnp.log2(size))
    mantissa = jnp.round(size * jnp.exp2(7.0 - power)) - 128.0
    power = jnp.where(mantissa > 127.0, power + 1.0, power) - 7.0
    mantissa = jnp.where(mantissa > 127.0, 0.0, mantissa)
    code = power * 256.0 + mantissa + jnp.where(values < 0, 128.0, 0.0)
    return jnp.where(tiny, -32768.0, code).astype(jnp.int16)


def gather_planes(orbitals):
    count, mine = orbitals.shape[:2]
    lines = CHUNK // 128
    steps = FOLD // CHUNK
    codes = encode(orbitals).reshape(count, mine, 2, steps, lines, 128)
    codes = jnp.transpose(codes, (3, 1, 0, 2, 4, 5)).reshape(-1, 128)
    codes = lax.all_gather(codes, "zh", axis=0)
    codes = lax.all_gather(codes, ("y", "x"), axis=0)
    return codes.reshape(32, steps, mine, 2 * count * lines, 128)


def columns_and_rows(cols, rows):
    sent = lax.all_to_all(rows, VAL + COND, 0, 0, tiled=True)
    line = lax.all_to_all(cols, ("zh",) + VAL, 0, 0, tiled=True)
    return lax.all_gather(line, ("y", "x"), axis=0), sent.reshape((4, 16, 2) + rows.shape[1:])


def per_device(
    valence_orbitals, conduction_orbitals, valence_energy, conduction_energy, sphere_index
):
    coded = pair_coefficients(
        gather_planes(valence_orbitals),
        conduction_orbitals,
        plane_tables(),
        line_tables(),
        sphere_index,
        (valence_energy, conduction_energy),
    )
    return pair_product(*columns_and_rows(*coded))


def solution(mesh):
    names = ("zl", "core", "y", "x", "zh")
    fine = Mesh(mesh.devices.reshape(2, 2, 4, 4, 2), names)
    placed = (P(VAL, COND, None), P(COND, None, None), P(VAL), P(COND), P())
    return jax.shard_map(
        per_device,
        mesh=fine,
        in_specs=placed,
        out_specs=(P(COND, VAL), P(COND, VAL)),
        check_vma=False,
    )
```
